256 devices in a mesh: dp: 16 (over y, z_lo, core), ctx: 16 (over x, z_hi).
Axes of the slice: x: 4, y: 4, z: 8 (z_hi: 4, z_lo: 2; z = z_hi * 2 + z_lo), core: 2. Of those that a mesh axis runs over, the one named last changes fastest.
Arguments:
- layer_input: bfloat16 [32768, 8192], P(('dp', 'ctx')), may hold values from -24 to 24
- queries: bfloat16 [32768, 4096], P(('dp', 'ctx')), may hold values from -8 to 8
- layer_keys: bfloat16 [32768, 512], P(('dp', 'ctx')), may hold values from -8 to 8
- layer_values: bfloat16 [32768, 512], P(('dp', 'ctx')), may hold values from -6 to 6
- output_grad: bfloat16 [32768, 4096], P(('dp', 'ctx')), may hold values from -6 to 6
- segment_ids: int32 [16, 2048], P('dp'), may hold values from 0 to 7, never falling along the last dimension, each value on 1 to 512 neighbouring positions
- first_moment: float32 [8192, 512], P(('dp', 'ctx')), may hold values from -112 to 112
- second_moment: float32 [8192, 512], P(('dp', 'ctx')), may hold values from 16.384 to 163.84
Outputs:
- attention: bfloat16 [32768, 4096], P(('dp', 'ctx'))
- query_grad: bfloat16 [32768, 4096], P(('dp', 'ctx'))
- key_grad: bfloat16 [32768, 512], P(('dp', 'ctx'))
- projection_update: bfloat16 [8192, 512], P('dp')
The draws below stay inside these ranges and needn't reach their ends.
Inputs may be any that keep to these rules, and one draw needn't show every extreme that they name: `segment_ids`: within each window the ids never fall; each rollout covers 1 to 512 positions, one exactly 512.
All inputs are finite; a program needn't handle non-finite values.
Results may differ from the reference program's by a relative error of at most 0.015.
Values may be sent and summed in bfloat16 or wider, within the bound.
A program may use at most 128 MiB of HBM per device.

```python
import math
import jax
import jax.numpy as jnp
import numpy as np
from jax import lax

D = 8192
HQ = 32
HK = 4
HD = 128
LENGTH = 2048
TOKENS = 32768
N_DP = 16
N_CTX = 16


def draw_queries(key, part):
    key = jax.random.fold_in(key, 11)
    drawn = jnp.clip(jax.random.normal(key, (TOKENS, HQ * HD), jnp.float32), -6.0, 6.0)
    return drawn.astype(jnp.bfloat16)


def draw_layer_keys(key, part):
    key = jax.random.fold_in(key, 23)
    drawn = jnp.clip(jax.random.normal(key, (TOKENS, HK * HD), jnp.float32), -6.0, 6.0)
    return drawn.astype(jnp.bfloat16)


def strengthened(values, stream_key, source, target, blocks, factor):
    def block_of(axis_at):
        return (jnp.arange(values.shape[axis_at]) // (values.shape[axis_at] // blocks)).reshape((-1,) + (1,) * (values.ndim - 1 - axis_at))

    first = jax.random.permutation(stream_key, blocks)[block_of(target)]
    other_side = (block_of(target) + blocks // 2) % blocks
    return jnp.where((block_of(source) == first) | (block_of(source) == other_side), factor * values, values)


def levels(rng, shape, split, smallest, high):
    def one(dim, shards_of):
        draws = jax.random.uniform(jax.random.fold_in(jax.random.fold_in(rng, 6), dim), (shards_of,), jnp.float32, smallest / len(split), high / len(split))
        return jnp.repeat(jnp.exp(draws), shape[dim] // shards_of).reshape((-1,) + (1,) * (len(shape) - dim - 1))

    gain = one(*split[0])
    for cut in split[1:]:
        gain = gain * one(*cut)
    return gain


def length_profile(number_of, total, reach, skew):
    portions = [(1 << 20) // math.isqrt(rank ** skew) + 1 for rank in range(2, number_of + 1)]
    surplus, given = total - reach - (number_of - 1), [1] * (number_of - 1)
    while surplus > 0:
        movable = [i for i in range(number_of - 1) if given[i] < reach]
        whole, left = sum([portions[i] for i in movable]), surplus
        for i in movable:
            more = min(reach - given[i], max(1, left * portions[i] // whole), surplus)
            given[i] = given[i] + more
            surplus = surplus - more
    return np.array([reach] + given)


def uneven_parts(rng, number_of, total, most, lean):
    if number_of == 2:
        one = jax.random.randint(rng, (), max(1, total - most), min(most, total - 1) + 1)
        return jnp.stack([one, total - one])
    tallies = jnp.asarray(length_profile(number_of, total, most, lean), jnp.int32)
    couples = (number_of - 1) // 2
    source_of, taker = tallies[1:1 + 2 * couples:2], tallies[2:2 + 2 * couples:2]
    margin = jnp.minimum(source_of - 1, most - taker)
    shifted = jax.random.randint(jax.random.fold_in(rng, 1), (couples,), 0, 1 << 20) % (margin + 1)
    tallies = tallies.at[1:1 + 2 * couples:2].set(source_of - shifted).at[2:2 + 2 * couples:2].set(taker + shifted)
    return tallies[jax.random.permutation(jax.random.fold_in(rng, 2), number_of)]


def scatter_about(stream_key, shape, deviation, bound, pieces=(), kind=jnp.bfloat16):
    values = deviation * jax.random.normal(stream_key, shape, jnp.float32)
    if pieces:
        values = values * levels(stream_key, shape, pieces, -0.22, 0.18)
    return jnp.clip(values, -bound, bound).astype(kind)


def gaussian_with(stream_key, shape, deviation, bound, shards, heavy, kind=jnp.bfloat16):
    values = deviation * jax.random.normal(stream_key, shape, jnp.float32)
    if shards:
        values = values * levels(stream_key, shape, shards, -0.22, 0.18)
    return jnp.clip(strengthened(values, jax.random.fold_in(stream_key, 3), *heavy), -bound, bound).astype(kind)


def setup_inputs(seed: int = 0) -> dict:
    seeds = jax.random.split(jax.random.key(seed), 9)
    layer_input = gaussian_with(seeds[0], (TOKENS, D), 1.0, 24.0, ((0, 256),), (0, 1, 256, 6.0))
    queries = draw_queries(jax.random.fold_in(seeds[8], 71), 0)
    layer_keys = draw_layer_keys(jax.random.fold_in(seeds[8], 71), 0)
    layer_values = scatter_about(seeds[3], (TOKENS, HK * HD), 1.0, 6.0, ((0, 256),))
    output_grad = scatter_about(seeds[4], (TOKENS, HQ * HD), 1.0, 6.0, ((0, 256),))
    segment_ids = jax.vmap(lambda own: jnp.searchsorted(jnp.cumsum(uneven_parts(own, max(8, LENGTH // 256), LENGTH, LENGTH // 4, 2)), jnp.arange(LENGTH), side="right"))(jax.random.split(seeds[5], N_DP)).reshape((N_DP, LENGTH)).astype(jnp.int32)
    first_moment = scatter_about(seeds[6], (D, HK * HD), (0.1 * TOKENS ** 0.5), 112.0, ((0, 256),), jnp.float32)
    second_moment = jnp.clip(jnp.exp(math.log(163.84) - 2.30258502 * jax.random.uniform(seeds[7], (D, HK * HD), jnp.float32) ** levels(seeds[7], (D, HK * HD), ((0, 256),), -0.2, 0.2)), 16.384, 163.84)
    return {"layer_input": layer_input, "queries": queries, "layer_keys": layer_keys, "layer_values": layer_values, "output_grad": output_grad, "segment_ids": segment_ids, "first_moment": first_moment, "second_moment": second_moment}


first_fix = 1.0 - 0.9 ** 8
second_fix = 1.0 - 0.999 ** 8

def one_window(parts):
    win_queries, win_keys, win_values, win_grads, segments = parts
    scaling = HD ** (-0.5)
    group = HQ // HK
    position = jnp.arange(LENGTH, dtype=jnp.int32)
    allowed = (position[None, :] <= position[:, None]) & (segments[:, None] == segments[None, :])

    def one_head(head):
        kv_head = (head // group).astype(jnp.int32)
        q_head = lax.dynamic_index_in_dim(win_queries, head, 1, keepdims=False)
        k_head = lax.dynamic_index_in_dim(win_keys, kv_head, 1, keepdims=False)
        v_head = lax.dynamic_index_in_dim(win_values, kv_head, 1, keepdims=False)
        g_head = lax.dynamic_index_in_dim(win_grads, head, 1, keepdims=False)
        raw = jnp.dot(q_head, k_head.T, preferred_element_type=jnp.float32) * scaling
        masked = jnp.where(allowed, raw, -1e+30)
        row_top = lax.optimization_barrier(jnp.max(masked, axis=1))
        row_total = lax.optimization_barrier(jnp.sum(jnp.where(allowed, jnp.exp(masked - row_top[:, None]), 0.0), axis=1))
        log_total = row_top + jnp.log(row_total)
        probs = jnp.where(allowed, jnp.exp(masked - log_total[:, None]), 0.0)
        probs_low = probs.astype(jnp.bfloat16)
        attended = jnp.dot(probs_low, v_head, preferred_element_type=jnp.float32).astype(jnp.bfloat16)
        delta = lax.optimization_barrier(jnp.sum(g_head.astype(jnp.float32) * attended.astype(jnp.float32), axis=1))
        dprobs = jnp.dot(g_head, v_head.T, preferred_element_type=jnp.float32)
        dscores = (probs * (dprobs - delta[:, None])).astype(jnp.bfloat16)
        dquery = (jnp.dot(dscores, k_head, preferred_element_type=jnp.float32) * scaling).astype(jnp.bfloat16)
        dkey = jnp.dot(dscores.T, q_head, preferred_element_type=jnp.float32) * scaling
        dvalue = jnp.dot(probs_low.T, g_head, preferred_element_type=jnp.float32)
        return (attended, dquery, dkey, dvalue)
    return lax.map(one_head, jnp.arange(HQ, dtype=jnp.int32))

def combine_parts(per_head):
    per_dev = HQ // N_CTX
    repeats = N_CTX // HK
    shaped = per_head.reshape(N_DP, HK, repeats, per_dev, LENGTH, HD)
    partial_value = lax.optimization_barrier(jnp.sum(shaped, axis=3)).astype(jnp.bfloat16)
    summed = lax.optimization_barrier(jnp.sum(partial_value.astype(jnp.float32), axis=2)).astype(jnp.bfloat16)
    return summed.transpose(0, 2, 1, 3).reshape(TOKENS, HK * HD)

def reference(layer_input, queries, layer_keys, layer_values, output_grad, segment_ids, first_moment, second_moment):
    windows = (queries.reshape(N_DP, LENGTH, HQ, HD), layer_keys.reshape(N_DP, LENGTH, HK, HD), layer_values.reshape(N_DP, LENGTH, HK, HD), output_grad.reshape(N_DP, LENGTH, HQ, HD), segment_ids)
    attended, dquery, dkey, dvalue = lax.map(one_window, windows)
    attention = attended.transpose(0, 2, 1, 3).reshape(TOKENS, HQ * HD)
    query_grad = dquery.transpose(0, 2, 1, 3).reshape(TOKENS, HQ * HD)
    key_grad = combine_parts(dkey)
    value_grad = combine_parts(dvalue)
    gradient = jnp.dot(layer_input.T, value_grad, preferred_element_type=jnp.float32)
    new_first = 0.9 * first_moment + 0.1 * gradient
    new_second = 0.999 * second_moment + 0.001 * gradient * gradient
    update = new_first / first_fix / (jnp.sqrt(new_second / second_fix) + 1e-08)
    return (attention, query_grad, key_grad, update.astype(jnp.bfloat16))
```

```python
import functools

import jax
import jax.numpy as jnp
from jax import lax
from jax.experimental import pallas as pl
from jax.experimental.pallas import tpu as pltpu
from jax.sharding import PartitionSpec as P

HQ = 32
HK = 4
HD = 128
GROUP = HQ // HK
BLK = 128
NB = 5
SPAN = NB * BLK
WIDE = 2 * HD
SCALE = HD**-0.5
LOG2E = 1.4426950408889634

first_fix = 1.0 - 0.9**8
second_fix = 1.0 - 0.999**8

NT = (((1,), (1,)), ((), ()))


def build_bias(me, n_ctx, seg_ref, bias_ref):
    rows = lax.broadcasted_iota(jnp.int32, (BLK, BLK), 0)
    cols = lax.broadcasted_iota(jnp.int32, (BLK, BLK), 1)
    own = seg_ref[0:1, pl.ds(pl.multiple_of(me * BLK, BLK), BLK)]
    for slot in range(NB):
        back = NB - 1 - slot
        block = lax.rem(me - back + n_ctx, n_ctx)
        theirs = seg_ref[0:1, pl.ds(pl.multiple_of(block * BLK, BLK), BLK)]
        column = jnp.sum(
            jnp.where(rows == cols, jnp.broadcast_to(theirs, (BLK, BLK)), 0).astype(jnp.float32),
            axis=1,
            keepdims=True,
        )
        allowed = column == own.astype(jnp.float32)
        if back == 0:
            allowed = allowed & (rows <= cols)
        else:
            allowed = allowed & (jnp.full((BLK, BLK), me, jnp.int32) >= back)
        bias = jnp.where(allowed, 0.0, -1e30)
        bias_ref[slot * BLK : (slot + 1) * BLK, 0:HD] = bias
        bias_ref[slot * BLK : (slot + 1) * BLK, HD:WIDE] = bias


def lanes(index):
    return pl.ds(pl.multiple_of(index * HD, HD), HD)


def pair_rows(ref, head):
    return jnp.concatenate([ref[:, lanes(head)], ref[:, lanes(head + 1)]], axis=0)


def group_rows(ref, g):
    return jnp.concatenate([ref[:, lanes(g * GROUP + i)] for i in range(GROUP)], axis=0)


def probs_of_group(g, q_ref, k_ref, bias_ref, prob_ref):
    k_head = k_ref[:, lanes(g)]
    for pair in range(GROUP // 2):
        head = g * GROUP + 2 * pair
        raw = lax.dot_general(
            k_head, pair_rows(q_ref, head), NT, preferred_element_type=jnp.float32
        )
        masked = raw + bias_ref[...]
        top = jnp.max(masked, axis=0, keepdims=True)
        grown = jnp.exp2((masked - top) * (SCALE * LOG2E))
        total = jnp.sum(grown, axis=0, keepdims=True)
        probs = grown * (1.0 / total)
        prob_ref[g, :, pair * WIDE : (pair + 1) * WIDE] = probs.astype(jnp.bfloat16)


def value_part(g, prob_ref, go_ref):
    return jnp.dot(prob_ref[g], group_rows(go_ref, g), preferred_element_type=jnp.float32)


def grads_of_group(g, q_ref, k_ref, v_ref, go_ref, prob_ref, ds_ref, out_ref, dq_ref):
    k_head = k_ref[:, lanes(g)]
    v_head = v_ref[:, lanes(g)]
    k_turned = k_head.T
    v_turned = v_head.T
    for pair in range(GROUP // 2):
        head = g * GROUP + 2 * pair
        cut = slice(pair * WIDE, (pair + 1) * WIDE)
        low = prob_ref[g, :, cut]
        dprobs = lax.dot_general(
            v_head, pair_rows(go_ref, head), NT, preferred_element_type=jnp.float32
        )
        probs = low.astype(jnp.float32)
        delta = jnp.sum(probs * dprobs, axis=0, keepdims=True)
        ds = (probs * (dprobs - delta)).astype(jnp.bfloat16)
        ds_ref[:, cut] = ds
        out_t = jnp.dot(v_turned, low, preferred_element_type=jnp.float32)
        dq_t = jnp.dot(k_turned, ds, preferred_element_type=jnp.float32) * SCALE
        for i in range(2):
            part = slice(i * HD, (i + 1) * HD)
            out_ref[:, lanes(head + i)] = out_t[:, part].T.astype(jnp.bfloat16)
            dq_ref[:, lanes(head + i)] = dq_t[:, part].T.astype(jnp.bfloat16)
    return (
        jnp.dot(ds_ref[...], group_rows(q_ref, g), preferred_element_type=jnp.float32) * SCALE
    )


def attention_kernel(
    n_ctx, q_ref, k_ref, v_ref, go_ref, seg_ref, out_ref, dq_ref, dk_ref, dv_ref,
    bias_ref, prob_ref, ds_ref,
):
    me = lax.axis_index("ctx")
    build_bias(me, n_ctx, seg_ref, bias_ref)

    @pl.loop(0, HK)
    def _(g):
        probs_of_group(g, q_ref, k_ref, bias_ref, prob_ref)
        dv_ref[:, lanes(g)] = value_part(g, prob_ref, go_ref).astype(jnp.bfloat16)

    @pl.loop(0, HK)
    def _(g):
        dk = grads_of_group(
            g, q_ref, k_ref, v_ref, go_ref, prob_ref, ds_ref, out_ref, dq_ref
        )
        dk_ref[:, lanes(g)] = dk.astype(jnp.bfloat16)


def attend(q, k, v, go, seg, n_ctx):
    bf = jnp.bfloat16
    whole = pl.BlockSpec(memory_space=pltpu.VMEM)
    return pl.pallas_call(
        functools.partial(attention_kernel, n_ctx),
        out_shape=(
            jax.ShapeDtypeStruct(q.shape, bf),
            jax.ShapeDtypeStruct(q.shape, bf),
            jax.ShapeDtypeStruct((SPAN, HK * HD), bf),
            jax.ShapeDtypeStruct((SPAN, HK * HD), bf),
        ),
        in_specs=[whole] * 5,
        out_specs=(whole,) * 4,
        scratch_shapes=[
            pltpu.VMEM((SPAN, WIDE), jnp.float32),
            pltpu.VMEM((HK, SPAN, GROUP * HD), bf),
            pltpu.VMEM((SPAN, GROUP * HD), bf),
        ],
        compiler_params=pltpu.CompilerParams(vmem_limit_bytes=48 * 1024 * 1024),
        cost_estimate=pl.CostEstimate(
            flops=2 * 6 * HQ * BLK * SPAN * HD, bytes_accessed=8 << 20, transcendentals=HQ * BLK * SPAN
        ),
    )(q, k, v, go, seg)


def body(
    layer_input, queries, layer_keys, layer_values, output_grad, segment_ids, first_moment, second_moment
):
    n_ctx = lax.axis_size("ctx")
    tok = queries.shape[0]

    def shifted(x, by):
        return lax.ppermute(x, "ctx", [(i, (i + by) % n_ctx) for i in range(n_ctx)])

    both = jnp.concatenate([layer_keys, layer_values], axis=1)
    spans = [shifted(both, by) for by in range(NB - 1, 0, -1)] + [both]
    spans = jnp.concatenate(spans, axis=0)
    k_span, v_span = spans[:, : HK * HD], spans[:, HK * HD :]
    inputs = lax.all_to_all(layer_input, "dp", split_axis=1, concat_axis=0, tiled=True)
    attention, query_grad, dk_part, dv_part = attend(
        queries, k_span, v_span, output_grad, segment_ids, n_ctx
    )
    parts = jnp.concatenate([dk_part, dv_part], axis=1)
    total = parts[(NB - 1) * tok :].astype(jnp.float32)
    for by in range(1, NB):
        slot = NB - 1 - by
        total = total + shifted(parts[slot * tok : (slot + 1) * tok], -by).astype(jnp.float32)
    total = total.astype(jnp.bfloat16)
    key_grad, value_grad = total[:, : HK * HD], total[:, HK * HD :]
    values_all = lax.all_gather(value_grad, "dp", axis=0, tiled=True)
    partial = lax.dot_general(
        inputs, values_all, (((0,), (0,)), ((), ())), preferred_element_type=jnp.float32
    )
    gradient = lax.psum_scatter(partial, "ctx", scatter_dimension=0, tiled=True)
    new_first = 0.9 * first_moment + 0.1 * gradient
    new_second = 0.999 * second_moment + 0.001 * gradient * gradient
    update = (new_first / first_fix / (jnp.sqrt(new_second / second_fix) + 1e-08)).astype(
        jnp.bfloat16
    )
    projection_update = lax.all_gather(update, "ctx", axis=0, tiled=True)
    return (attention, query_grad, key_grad, projection_update)


def solution(mesh):
    rows = P(("dp", "ctx"), None)
    in_specs = (rows, rows, rows, rows, rows, P("dp", None), rows, rows)
    out_specs = (rows, rows, rows, P("dp", None))
    return jax.shard_map(body, mesh=mesh, in_specs=in_specs, out_specs=out_specs, check_vma=False)
```

```python
import jax
import jax.numpy as jnp
from jax import lax
from jax.experimental import pallas as pl
from jax.experimental.pallas import tpu as pltpu
from jax.sharding import PartitionSpec as P

HQ = 32
HK = 4
HD = 128
GROUP = HQ // HK
BLK = 128
NB = 5
SPAN = NB * BLK
WIDE = 2 * HD
SCALE = HD**-0.5
LOG2E = 1.4426950408889634

first_fix = 1.0 - 0.9**8
second_fix = 1.0 - 0.999**8

NT = (((1,), (1,)), ((), ()))


def build_bias(me, n_ctx, seg_ref, bias_ref):
    rows = lax.broadcasted_iota(jnp.int32, (BLK, BLK), 0)
    cols = lax.broadcasted_iota(jnp.int32, (BLK, BLK), 1)
    own = seg_ref[0:1, pl.ds(pl.multiple_of(me * BLK, BLK), BLK)]
    for slot in range(NB):
        back = NB - 1 - slot
        block = lax.rem(me - back + n_ctx, n_ctx)
        theirs = seg_ref[0:1, pl.ds(pl.multiple_of(block * BLK, BLK), BLK)]
        column = jnp.sum(
            jnp.where(rows == cols, jnp.broadcast_to(theirs, (BLK, BLK)), 0).astype(jnp.float32),
            axis=1,
            keepdims=True,
        )
        allowed = column == own.astype(jnp.float32)
        if back == 0:
            allowed = allowed & (rows <= cols)
        else:
            allowed = allowed & (jnp.full((BLK, BLK), me, jnp.int32) >= back)
        bias = jnp.where(allowed, 0.0, -1e30)
        bias_ref[slot * BLK : (slot + 1) * BLK, 0:HD] = bias
        bias_ref[slot * BLK : (slot + 1) * BLK, HD:WIDE] = bias


def lanes(index):
    return pl.ds(pl.multiple_of(index * HD, HD), HD)


def pair_rows(ref, head):
    return jnp.concatenate([ref[:, lanes(head)], ref[:, lanes(head + 1)]], axis=0)


def group_rows(ref, g):
    return jnp.concatenate([ref[:, lanes(g * GROUP + i)] for i in range(GROUP)], axis=0)


def probs_of_group(g, q_ref, k_ref, bias_ref, prob_ref):
    k_head = k_ref[:, lanes(g)]
    for pair in range(GROUP // 2):
        head = g * GROUP + 2 * pair
        raw = lax.dot_general(
            k_head, pair_rows(q_ref, head), NT, preferred_element_type=jnp.float32
        )
        masked = raw + bias_ref[...]
        top = jnp.max(masked, axis=0, keepdims=True)
        grown = jnp.exp2((masked - top) * (SCALE * LOG2E))
        total = jnp.sum(grown, axis=0, keepdims=True)
        probs = grown * (1.0 / total)
        prob_ref[g, :, pair * WIDE : (pair + 1) * WIDE] = probs.astype(jnp.bfloat16)


def value_part(g, prob_ref, go_ref):
    return jnp.dot(prob_ref[g], group_rows(go_ref, g), preferred_element_type=jnp.float32)


def grads_of_group(g, q_ref, k_ref, v_ref, go_ref, prob_ref, ds_ref, out_ref, dq_ref):
    k_head = k_ref[:, lanes(g)]
    v_head = v_ref[:, lanes(g)]
    k_turned = k_head.T
    v_turned = v_head.T
    for pair in range(GROUP // 2):
        head = g * GROUP + 2 * pair
        cut = slice(pair * WIDE, (pair + 1) * WIDE)
        low = prob_ref[g, :, cut]
        dprobs = lax.dot_general(
            v_head, pair_rows(go_ref, head), NT, preferred_element_type=jnp.float32
        )
        probs = low.astype(jnp.float32)
        delta = jnp.sum(probs * dprobs, axis=0, keepdims=True)
        ds = (probs * (dprobs - delta)).astype(jnp.bfloat16)
        ds_ref[:, cut] = ds
        out_t = jnp.dot(v_turned, low, preferred_element_type=jnp.float32)
        dq_t = jnp.dot(k_turned, ds, preferred_element_type=jnp.float32) * SCALE
        for i in range(2):
            part = slice(i * HD, (i + 1) * HD)
            out_ref[:, lanes(head + i)] = out_t[:, part].T.astype(jnp.bfloat16)
            dq_ref[:, lanes(head + i)] = dq_t[:, part].T.astype(jnp.bfloat16)
    return (
        jnp.dot(ds_ref[...], group_rows(q_ref, g), preferred_element_type=jnp.float32) * SCALE
    )


MESH = pl.DeviceIdType.MESH
N_CTX = 16
N_X = 4
N_ZH = 4
N_Y = 4
ROWS = 32
WIDTH = HK * HD


def remote(src, dst, send_sem, recv_sem, dp, ctx):
    return pltpu.make_async_remote_copy(
        src_ref=src,
        dst_ref=dst,
        send_sem=send_sem,
        recv_sem=recv_sem,
        device_id=(dp, ctx),
        device_id_type=MESH,
    )


def step_kernel(
    x_ref, q_ref, k_ref, v_ref, go_ref, seg_ref, m_ref, s_ref,
    out_ref, dq_ref, dk_ref, up_ref,
    bias_ref, prob_ref, ds_ref, out_v, dq_v, k_span, v_span, dv_part, dk_part, dv_got, dk_got,
    xs_ref, xt_ref, vg_ref, sx_ref, rx_ref, acc_ref, sz_ref, rz_ref, up_v,
    halo_s, halo_r, x_s, x_r, x_l, dv_s, dv_r, dk_s, dk_r, vg_s, vg_r,
    rx_s, rx_r, rz_s, rz_r, ag_s, ag_r, out_l,
):
    bf = jnp.bfloat16
    dp = lax.axis_index("dp")
    me = lax.axis_index("ctx")
    y, zl, core = dp // 4, (dp // 2) % 2, dp % 2
    x, zh = me // N_ZH, me % N_ZH

    def ctx_at(by):
        return (me + by + N_CTX) % N_CTX

    def share_at(dy, dc):
        return ((y + dy) % N_Y) * 4 + zl * 2 + (core + dc) % 2

    def x_at(dx):
        return ((x + dx) % N_X) * N_ZH + zh

    def z_at(dh):
        return x * N_ZH + (zh + dh) % N_ZH

    def zl_at(dl):
        return y * 4 + ((zl + dl) % 2) * 2 + core

    partners = [(dp, ctx_at(by)) for by in (1, 2, 3, 4, -1, -2, -3, -4, 8)]
    partners += [(share_at(e // 2, e % 2), me) for e in range(1, 8)]
    partners += [(zl_at(1), z_at(dh)) for dh in range(N_ZH)]
    barrier = pltpu.get_barrier_semaphore()
    for partner in partners:
        pl.semaphore_signal(barrier, inc=1, device_id=partner, device_id_type=MESH)
    pl.semaphore_wait(barrier, len(partners))

    def halo(which, by):
        src, span = ((k_ref, k_span), (v_ref, v_span))[which]
        slot = NB - 1 - by
        return remote(
            src,
            span.at[pl.ds(slot * BLK, BLK), :],
            halo_s.at[which, by - 1],
            halo_r.at[which, by - 1],
            dp,
            ctx_at(by),
        )

    def x_share(e, j):
        dy, dc = e // 2, e % 2
        first = (((y + dy) % N_Y) * 4 + j * 2 + (core + dc) % 2) * 512
        src = x_ref.at[:, pl.ds(pl.multiple_of(first, 512), 512)]
        dst = xs_ref.at[e, :, pl.ds(j * 512, 512)]
        if e == 0:
            return pltpu.make_async_copy(src, dst, x_l.at[j])
        return remote(src, dst, x_s.at[e, j], x_r.at[e, j], share_at(dy, dc), me)

    for which in range(2):
        for by in range(1, NB):
            halo(which, by).start()
    for e in (1, 2, 3, 6, 7, 4, 5, 0):
        for j in range(2):
            x_share(e, j).start()

    k_span[(NB - 1) * BLK :, :] = k_ref[...]
    v_span[(NB - 1) * BLK :, :] = v_ref[...]
    build_bias(me, N_CTX, seg_ref, bias_ref)

    def back(part, got, send, recv, g, by):
        slot = NB - 1 - by
        return remote(
            part.at[pl.ds(slot * BLK, BLK), lanes(g)],
            got.at[by - 1, :, lanes(g)],
            send.at[g, by - 1],
            recv.at[g, by - 1],
            dp,
            ctx_at(-by),
        )

    for by in range(1, NB):
        halo(0, by).wait_recv()

    @pl.loop(0, HK)
    def _(g):
        probs_of_group(g, q_ref, k_span, bias_ref, prob_ref)
        dv_part[:, lanes(g)] = value_part(g, prob_ref, go_ref).astype(bf)
        for by in range(1, NB):
            back(dv_part, dv_got, dv_s, dv_r, g, by).start()

    for by in range(1, NB):
        halo(1, by).wait_recv()

    def grads(first, last):
        @pl.loop(first, last)
        def _(g):
            dk = grads_of_group(
                g, q_ref, k_span, v_span, go_ref, prob_ref, ds_ref, out_v, dq_v
            )
            dk_part[:, lanes(g)] = dk.astype(bf)
            for by in range(1, NB):
                back(dk_part, dk_got, dk_s, dk_r, g, by).start()

    grads(0, 2)

    def gathered(part, got, send, recv):
        @pl.loop(0, HK)
        def _(g):
            for by in range(1, NB):
                back(part, got, send, recv, g, by).wait_recv()
        total = part[(NB - 1) * BLK :, :].astype(jnp.float32)
        for by in range(1, NB):
            total = total + got[by - 1].astype(jnp.float32)
        return total.astype(bf)

    vg_ref[0] = gathered(dv_part, dv_got, dv_s, dv_r)

    def vg_send(dy):
        return remote(
            vg_ref.at[0], vg_ref.at[2 * dy], vg_s.at[2 * dy], vg_r.at[2 * dy], share_at(dy, 0), me
        )

    def vg_pass(dy):
        return remote(
            vg_ref.at[2 * dy],
            vg_ref.at[2 * dy + 1],
            vg_s.at[2 * dy + 1],
            vg_r.at[2 * dy + 1],
            share_at(0, 1),
            me,
        )

    for dy in range(1, N_Y):
        vg_send(dy).start()
    vg_pass(0).start()

    for e in range(8):
        for j in range(2):
            if e == 0:
                x_share(e, j).wait()
            else:
                x_share(e, j).wait_recv()

    @pl.loop(0, 8)
    def _(e):
        xt_ref[:, lanes(e)] = xs_ref[e].T

    grads(2, HK)
    copies = (
        pltpu.make_async_copy(out_v, out_ref, out_l.at[0]),
        pltpu.make_async_copy(dq_v, dq_ref, out_l.at[1]),
    )
    for copy in copies:
        copy.start()

    for dy in range(1, N_Y):
        vg_send(dy).wait_recv()
        vg_pass(dy).start()
    for dy in range(N_Y):
        vg_pass(dy).wait_recv()

    def x_piece(d, j):
        return remote(
            sx_ref.at[d, pl.ds(j * 128, 128), :],
            rx_ref.at[d, pl.ds(j * 128, 128), :],
            rx_s.at[d, j],
            rx_r.at[d, j],
            dp,
            x_at(d),
        )

    def partial_for(d):
        first = ((x + d) % N_X) * 128
        left = jnp.concatenate(
            [xt_ref[pl.ds(pl.multiple_of(j * 512 + first, 128), 128), :] for j in range(2)], axis=0
        )
        return jnp.dot(
            left, vg_ref[...].reshape(8 * BLK, WIDTH), preferred_element_type=jnp.float32
        )

    for d in (2, 1, 3):
        sx_ref[d] = partial_for(d).astype(bf)
        for j in range(2):
            x_piece(d, j).start()
    acc_ref[...] = partial_for(0)

    for d in (2, 1, 3):
        for j in range(2):
            x_piece(d, j).wait_recv()
    acc_ref[...] = (
        acc_ref[...]
        + rx_ref[1].astype(jnp.float32)
        + rx_ref[2].astype(jnp.float32)
        + rx_ref[3].astype(jnp.float32)
    )
    sz_ref[...] = acc_ref[...].astype(bf)

    def z_rows(dl, dh):
        first = ((zl + dl) % 2) * 128 + ((zh + dh) % N_ZH) * ROWS
        return pl.ds(pl.multiple_of(first, ROWS), ROWS)

    def z_piece(e):
        dl, dh = e % 2, e // 2
        return remote(
            sz_ref.at[z_rows(dl, dh), :], rz_ref.at[e], rz_s.at[e], rz_r.at[e], zl_at(dl), z_at(dh)
        )

    for e in (4, 5, 3, 2, 6, 7, 1):
        z_piece(e).start()

    dk_ref[...] = gathered(dk_part, dk_got, dk_s, dk_r)

    for e in range(1, 8):
        z_piece(e).wait_recv()
    gradient = acc_ref[z_rows(0, 0), :]
    for e in range(1, 8):
        gradient = gradient + rz_ref[e].astype(jnp.float32)
    new_first = 0.9 * m_ref[...] + 0.1 * gradient
    new_second = 0.999 * s_ref[...] + 0.001 * gradient * gradient
    update = new_first / first_fix / (jnp.sqrt(new_second / second_fix) + 1e-08)

    def up_rows(dh):
        return up_v.at[pl.ds(pl.multiple_of(z_at(dh) * ROWS, ROWS), ROWS), :]

    up_v[pl.ds(pl.multiple_of(me * ROWS, ROWS), ROWS), :] = update.astype(bf)

    def along_z(dh):
        return remote(up_rows(0), up_rows(0), ag_s.at[0, dh], ag_r.at[0, dh], dp, z_at(dh))

    def along_x(dx, dh):
        return remote(up_rows(-dh), up_rows(-dh), ag_s.at[dx, dh], ag_r.at[dx, dh], dp, x_at(dx))

    for dh in (2, 1, 3):
        along_z(dh).start()
    for dx in (2, 1, 3):
        along_x(dx, 0).start()
    for dh in (1, 3, 2):
        along_z(dh).wait_recv()
        for dx in (2, 1, 3):
            along_x(dx, dh).start()
    for dx in range(1, N_X):
        for dh in range(N_ZH):
            along_x(dx, dh).wait_recv()
    last = pltpu.make_async_copy(up_v, up_ref, out_l.at[2])
    last.start()

    for which in range(2):
        for by in range(1, NB):
            halo(which, by).wait_send()
    for e in range(1, 8):
        for j in range(2):
            x_share(e, j).wait_send()

    @pl.loop(0, HK)
    def _(g):
        for by in range(1, NB):
            back(dv_part, dv_got, dv_s, dv_r, g, by).wait_send()
            back(dk_part, dk_got, dk_s, dk_r, g, by).wait_send()

    for dy in range(1, N_Y):
        vg_send(dy).wait_send()
    for dy in range(N_Y):
        vg_pass(dy).wait_send()
    for d in range(1, N_X):
        for j in range(2):
            x_piece(d, j).wait_send()
    for e in range(1, 8):
        z_piece(e).wait_send()
    for dh in range(1, N_ZH):
        along_z(dh).wait_send()
    for dx in range(1, N_X):
        for dh in range(N_ZH):
            along_x(dx, dh).wait_send()
    for copy in copies:
        copy.wait()
    last.wait()


def body(
    layer_input, queries, layer_keys, layer_values, output_grad, segment_ids, first_moment, second_moment
):
    bf = jnp.bfloat16
    f32 = jnp.float32
    whole = pl.BlockSpec(memory_space=pltpu.VMEM)
    far = pl.BlockSpec(memory_space=pl.ANY)
    dma = pltpu.SemaphoreType.DMA
    return pl.pallas_call(
        step_kernel,
        out_shape=(
            jax.ShapeDtypeStruct(queries.shape, bf),
            jax.ShapeDtypeStruct(queries.shape, bf),
            jax.ShapeDtypeStruct(layer_keys.shape, bf),
            jax.ShapeDtypeStruct((N_CTX * ROWS, WIDTH), bf),
        ),
        in_specs=[far] + [whole] * 7,
        out_specs=(far, far, whole, far),
        scratch_shapes=[
            pltpu.VMEM((SPAN, WIDE), f32),
            pltpu.VMEM((HK, SPAN, GROUP * HD), bf),
            pltpu.VMEM((SPAN, GROUP * HD), bf),
            pltpu.VMEM((BLK, HQ * HD), bf),
            pltpu.VMEM((BLK, HQ * HD), bf),
            pltpu.VMEM((SPAN, WIDTH), bf),
            pltpu.VMEM((SPAN, WIDTH), bf),
            pltpu.VMEM((SPAN, WIDTH), bf),
            pltpu.VMEM((SPAN, WIDTH), bf),
            pltpu.VMEM((NB - 1, BLK, WIDTH), bf),
            pltpu.VMEM((NB - 1, BLK, WIDTH), bf),
            pltpu.VMEM((8, BLK, 1024), bf),
            pltpu.VMEM((1024, 8 * BLK), bf),
            pltpu.VMEM((8, BLK, WIDTH), bf),
            pltpu.VMEM((N_X, 256, WIDTH), bf),
            pltpu.VMEM((N_X, 256, WIDTH), bf),
            pltpu.VMEM((256, WIDTH), f32),
            pltpu.VMEM((256, WIDTH), bf),
            pltpu.VMEM((8, ROWS, WIDTH), bf),
            pltpu.VMEM((N_CTX * ROWS, WIDTH), bf),
            dma((2, NB - 1)),
            dma((2, NB - 1)),
            dma((8, 2)),
            dma((8, 2)),
            dma((2,)),
            dma((HK, NB - 1)),
            dma((HK, NB - 1)),
            dma((HK, NB - 1)),
            dma((HK, NB - 1)),
            dma((8,)),
            dma((8,)),
            dma((N_X, 2)),
            dma((N_X, 2)),
            dma((8,)),
            dma((8,)),
            dma((N_X, N_ZH)),
            dma((N_X, N_ZH)),
            dma((3,)),
        ],
        compiler_params=pltpu.CompilerParams(
            collective_id=0, has_side_effects=True, vmem_limit_bytes=48 * 1024 * 1024
        ),
        cost_estimate=pl.CostEstimate(
            flops=2 * 6 * HQ * BLK * SPAN * HD,
            bytes_accessed=8 << 20,
            transcendentals=HQ * BLK * SPAN,
        ),
    )(
        layer_input, queries, layer_keys, layer_values, output_grad, segment_ids, first_moment,
        second_moment,
    )


def solution(mesh):
    rows = P(("dp", "ctx"), None)
    in_specs = (rows, rows, rows, rows, rows, P("dp", None), rows, rows)
    out_specs = (rows, rows, rows, P("dp", None))
    return jax.shard_map(body, mesh=mesh, in_specs=in_specs, out_specs=out_specs, check_vma=False)
```

```python
import jax
import jax.numpy as jnp
from jax import lax
from jax.experimental import pallas as pl
from jax.experimental.pallas import tpu as pltpu
from jax.sharding import PartitionSpec as P

HQ = 32
HK = 4
HD = 128
GROUP = HQ // HK
BLK = 128
NB = 5
SPAN = NB * BLK
WIDE = 2 * HD
SCALE = HD**-0.5
LOG2E = 1.4426950408889634

first_fix = 1.0 - 0.9**8
second_fix = 1.0 - 0.999**8

NT = (((1,), (1,)), ((), ()))


def build_bias(me, n_ctx, seg_ref, bias_ref):
    rows = lax.broadcasted_iota(jnp.int32, (BLK, BLK), 0)
    cols = lax.broadcasted_iota(jnp.int32, (BLK, BLK), 1)
    own = seg_ref[0:1, pl.ds(pl.multiple_of(me * BLK, BLK), BLK)]
    for slot in range(NB):
        back = NB - 1 - slot
        block = lax.rem(me - back + n_ctx, n_ctx)
        theirs = seg_ref[0:1, pl.ds(pl.multiple_of(block * BLK, BLK), BLK)]
        column = jnp.sum(
            jnp.where(rows == cols, jnp.broadcast_to(theirs, (BLK, BLK)), 0).astype(jnp.float32),
            axis=1,
            keepdims=True,
        )
        allowed = column == own.astype(jnp.float32)
        if back == 0:
            allowed = allowed & (rows <= cols)
        else:
            allowed = allowed & (jnp.full((BLK, BLK), me, jnp.int32) >= back)
        bias = jnp.where(allowed, 0.0, -1e30)
        bias_ref[slot * BLK : (slot + 1) * BLK, 0:HD] = bias
        bias_ref[slot * BLK : (slot + 1) * BLK, HD:WIDE] = bias


def lanes(index):
    return pl.ds(pl.multiple_of(index * HD, HD), HD)


def pair_rows(ref, head):
    return jnp.concatenate([ref[:, lanes(head)], ref[:, lanes(head + 1)]], axis=0)


def group_rows(ref, g):
    return jnp.concatenate([ref[:, lanes(g * GROUP + i)] for i in range(GROUP)], axis=0)


def probs_of_group(g, q_ref, k_ref, bias_ref, prob_ref):
    k_head = k_ref[:, lanes(g)]
    for pair in range(GROUP // 2):
        head = g * GROUP + 2 * pair
        raw = lax.dot_general(
            k_head, pair_rows(q_ref, head), NT, preferred_element_type=jnp.float32
        )
        masked = raw + bias_ref[...]
        top = jnp.max(masked, axis=0, keepdims=True)
        grown = jnp.exp2((masked - top) * (SCALE * LOG2E))
        total = jnp.sum(grown, axis=0, keepdims=True)
        probs = grown * (1.0 / total)
        prob_ref[g, :, pair * WIDE : (pair + 1) * WIDE] = probs.astype(jnp.bfloat16)


def value_part(g, prob_ref, go_ref):
    return jnp.dot(prob_ref[g], group_rows(go_ref, g), preferred_element_type=jnp.float32)


def grads_of_group(g, q_ref, k_ref, v_ref, go_ref, prob_ref, ds_ref, out_ref, dq_ref):
    k_head = k_ref[:, lanes(g)]
    v_head = v_ref[:, lanes(g)]
    k_turned = k_head.T
    v_turned = v_head.T
    for pair in range(GROUP // 2):
        head = g * GROUP + 2 * pair
        cut = slice(pair * WIDE, (pair + 1) * WIDE)
        low = prob_ref[g, :, cut]
        dprobs = lax.dot_general(
            v_head, pair_rows(go_ref, head), NT, preferred_element_type=jnp.float32
        )
        probs = low.astype(jnp.float32)
        delta = jnp.sum(probs * dprobs, axis=0, keepdims=True)
        ds = (probs * (dprobs - delta)).astype(jnp.bfloat16)
        ds_ref[:, cut] = ds
        out_t = jnp.dot(v_turned, low, preferred_element_type=jnp.float32)
        dq_t = jnp.dot(k_turned, ds, preferred_element_type=jnp.float32) * SCALE
        for i in range(2):
            part = slice(i * HD, (i + 1) * HD)
            out_ref[:, lanes(head + i)] = out_t[:, part].T.astype(jnp.bfloat16)
            dq_ref[:, lanes(head + i)] = dq_t[:, part].T.astype(jnp.bfloat16)
    return (
        jnp.dot(ds_ref[...], group_rows(q_ref, g), preferred_element_type=jnp.float32) * SCALE
    )


MESH = pl.DeviceIdType.MESH
N_CTX = 16
N_X = 4
N_ZH = 4
N_Y = 4
ROWS = 32
WIDTH = HK * HD
HALF = WIDTH // 2


def remote(src, dst, send_sem, recv_sem, dp, ctx):
    return pltpu.make_async_remote_copy(
        src_ref=src,
        dst_ref=dst,
        send_sem=send_sem,
        recv_sem=recv_sem,
        device_id=(dp, ctx),
        device_id_type=MESH,
    )


def step_kernel(
    x_ref, q_hbm, k_hbm, v_hbm, go_hbm, seg_hbm, m_hbm, s_hbm,
    out_ref, dq_ref, dk_ref, up_ref,
    q_ref, go_ref, seg_ref, m_ref, s_ref,
    bias_ref, prob_ref, ds_ref, out_v, dq_v, k_span, v_span, dv_part, dk_part, dv_got, dk_got,
    xs_ref, xt_ref, vg_ref, sx_ref, rx_ref, acc_ref, sz_ref, rz_ref, up_v, dk_v,
    load_l, halo_s, halo_r, x_s, x_r, x_l, dv_s, dv_r, dk_s, dk_r, vg_s, vg_r,
    rx_s, rx_r, rz_s, rz_r, ag_s, ag_r, out_l,
):
    bf = jnp.bfloat16
    f32 = jnp.float32
    dp = lax.axis_index("dp")
    me = lax.axis_index("ctx")
    y, zl, core = dp // 4, (dp // 2) % 2, dp % 2
    x, zh = me // N_ZH, me % N_ZH
    own_rows = pl.ds((NB - 1) * BLK, BLK)

    loads = [
        pltpu.make_async_copy(src, dst, load_l.at[i])
        for i, (src, dst) in enumerate(
            (
                (seg_hbm, seg_ref),
                (k_hbm, k_span.at[own_rows, :]),
                (q_hbm, q_ref),
                (go_hbm, go_ref),
                (v_hbm, v_span.at[own_rows, :]),
                (m_hbm, m_ref),
                (s_hbm, s_ref),
            )
        )
    ]
    for load in loads:
        load.start()

    def ctx_at(by):
        return (me + by + N_CTX) % N_CTX

    def share_at(dy, dc):
        return ((y + dy) % N_Y) * 4 + zl * 2 + (core + dc) % 2

    def x_at(dx):
        return ((x + dx) % N_X) * N_ZH + zh

    def z_at(dh):
        return x * N_ZH + (zh + dh + N_ZH) % N_ZH

    def zl_at(dl):
        return y * 4 + ((zl + dl) % 2) * 2 + core

    partners = [(dp, ctx_at(by)) for by in (1, 2, 3, 4, -1, -2, -3, -4, 8)]
    partners += [(share_at(e // 2, e % 2), me) for e in range(1, 8)]
    partners += [(zl_at(1), z_at(dh)) for dh in range(N_ZH)]
    barrier = pltpu.get_barrier_semaphore()
    for partner in partners:
        pl.semaphore_signal(barrier, inc=1, device_id=partner, device_id_type=MESH)
    pl.semaphore_wait(barrier, len(partners))

    def halo(which, g, by):
        src, span = ((k_hbm, k_span), (v_hbm, v_span))[which]
        slot = NB - 1 - by
        return remote(
            src.at[:, lanes(g)],
            span.at[pl.ds(slot * BLK, BLK), lanes(g)],
            halo_s.at[which, g, by - 1],
            halo_r.at[which, g, by - 1],
            dp,
            ctx_at(by),
        )

    def x_share(e, j):
        dy, dc = e // 2, e % 2
        first = (((y + dy) % N_Y) * 4 + j * 2 + (core + dc) % 2) * 512
        src = x_ref.at[:, pl.ds(pl.multiple_of(first, 512), 512)]
        dst = xs_ref.at[e, :, pl.ds(j * 512, 512)]
        if e == 0:
            return pltpu.make_async_copy(src, dst, x_l.at[j])
        return remote(src, dst, x_s.at[e, j], x_r.at[e, j], share_at(dy, dc), me)

    def back(part, got, send, recv, g, by):
        slot = NB - 1 - by
        return remote(
            part.at[pl.ds(slot * BLK, BLK), lanes(g)],
            got.at[by - 1, :, lanes(g)],
            send.at[g, by - 1],
            recv.at[g, by - 1],
            dp,
            ctx_at(-by),
        )

    def dv_back(g, by):
        return back(dv_part, dv_got, dv_s, dv_r, g, by)

    def dk_back(g, by):
        return back(dk_part, dk_got, dk_s, dk_r, g, by)

    def send_spans(which, first, last):
        @pl.loop(first, last)
        def _(g):
            for by in range(1, NB):
                halo(which, g, by).start()

    def probs(first, last):
        @pl.loop(first, last)
        def _(g):
            for by in range(1, NB):
                halo(0, g, by).wait_recv()
            probs_of_group(g, q_ref, k_span, bias_ref, prob_ref)
            dv_part[:, lanes(g)] = value_part(g, prob_ref, go_ref).astype(bf)
            for by in range(1, NB):
                dv_back(g, by).start()

    def grads(first, last):
        @pl.loop(first, last)
        def _(g):
            for by in range(1, NB):
                halo(1, g, by).wait_recv()
            dk = grads_of_group(
                g, q_ref, k_span, v_span, go_ref, prob_ref, ds_ref, out_v, dq_v
            )
            dk_part[:, lanes(g)] = dk.astype(bf)
            for by in range(1, NB):
                dk_back(g, by).start()

    def columns(h):
        return pl.ds(h * HALF, HALF)

    def sum_values(h):
        for g in (2 * h, 2 * h + 1):
            for by in range(1, NB):
                dv_back(g, by).wait_recv()
        total = dv_part[own_rows, columns(h)].astype(f32)
        for by in range(1, NB):
            total = total + dv_got[by - 1, :, columns(h)].astype(f32)
        vg_ref[h, 0] = total.astype(bf)

    def vg_send(h, dy):
        e = 2 * dy
        return remote(
            vg_ref.at[h, 0], vg_ref.at[h, e], vg_s.at[h, e], vg_r.at[h, e], share_at(dy, 0), me
        )

    def vg_pass(h, dy):
        e = 2 * dy
        return remote(
            vg_ref.at[h, e],
            vg_ref.at[h, e + 1],
            vg_s.at[h, e + 1],
            vg_r.at[h, e + 1],
            share_at(0, 1),
            me,
        )

    def gather_values(h):
        for dy in (2, 1, 3):
            vg_send(h, dy).start()
        vg_pass(h, 0).start()

    def pass_values(h):
        for dy in (1, 3, 2):
            vg_send(h, dy).wait_recv()
            vg_pass(h, dy).start()

    def turn_inputs():
        for e in range(8):
            for j in range(2):
                if e == 0:
                    x_share(e, j).wait()
                else:
                    x_share(e, j).wait_recv()

        @pl.loop(0, 8)
        def _(e):
            xt_ref[:, lanes(e)] = xs_ref[e].T

    def x_piece(h, d):
        return remote(
            sx_ref.at[h, d], rx_ref.at[h, d], rx_s.at[h, d], rx_r.at[h, d], dp, x_at(d)
        )

    def partial_for(h, d):
        first = ((x + d) % N_X) * 128
        left = jnp.concatenate(
            [xt_ref[pl.ds(pl.multiple_of(j * 512 + first, 128), 128), :] for j in range(2)], axis=0
        )
        return jnp.dot(left, vg_ref[h].reshape(8 * BLK, HALF), preferred_element_type=f32)

    def partials(h):
        for dy in range(N_Y):
            vg_pass(h, dy).wait_recv()
        for d in (2, 1, 3):
            sx_ref[h, d] = partial_for(h, d).astype(bf)
            x_piece(h, d).start()
        acc_ref[h] = partial_for(h, 0)

    def z_rows(dl, dh):
        first = ((zl + dl) % 2) * 128 + ((zh + dh) % N_ZH) * ROWS
        return pl.ds(pl.multiple_of(first, ROWS), ROWS)

    def z_piece(h, e):
        dl, dh = e % 2, e // 2
        return remote(
            sz_ref.at[h, z_rows(dl, dh), :],
            rz_ref.at[h, e],
            rz_s.at[h, e],
            rz_r.at[h, e],
            zl_at(dl),
            z_at(dh),
        )

    def sum_x(h):
        for d in (1, 3, 2):
            x_piece(h, d).wait_recv()
        total = acc_ref[h]
        for d in range(1, N_X):
            total = total + rx_ref[h, d].astype(f32)
        acc_ref[h] = total
        sz_ref[h] = total.astype(bf)
        for e in (4, 5, 3, 2, 6, 7, 1):
            z_piece(h, e).start()

    def up_rows(h, dh):
        return up_v.at[pl.ds(pl.multiple_of(z_at(dh) * ROWS, ROWS), ROWS), columns(h)]

    def along_z(h, dh):
        return remote(
            up_rows(h, 0), up_rows(h, 0), ag_s.at[h, 0, dh], ag_r.at[h, 0, dh], dp, z_at(dh)
        )

    def along_x(h, dx, dh):
        return remote(
            up_rows(h, -dh), up_rows(h, -dh), ag_s.at[h, dx, dh], ag_r.at[h, dx, dh], dp, x_at(dx)
        )

    def adam(h):
        for e in range(1, 8):
            z_piece(h, e).wait_recv()
        gradient = acc_ref[h, z_rows(0, 0), :]
        for e in range(1, 8):
            gradient = gradient + rz_ref[h, e].astype(f32)
        new_first = 0.9 * m_ref[:, columns(h)] + 0.1 * gradient
        new_second = 0.999 * s_ref[:, columns(h)] + 0.001 * gradient * gradient
        update = new_first / first_fix / (jnp.sqrt(new_second / second_fix) + 1e-08)
        up_v[pl.ds(pl.multiple_of(me * ROWS, ROWS), ROWS), columns(h)] = update.astype(bf)
        for dh in (2, 1, 3):
            along_z(h, dh).start()
        for dx in (2, 1, 3):
            along_x(h, dx, 0).start()

    def pass_updates(h):
        for dh in (1, 3, 2):
            along_z(h, dh).wait_recv()
            for dx in (2, 1, 3):
                along_x(h, dx, dh).start()

    def sum_keys():
        @pl.loop(0, HK)
        def _(g):
            for by in range(1, NB):
                dk_back(g, by).wait_recv()

        total = dk_part[own_rows, :].astype(f32)
        for by in range(1, NB):
            total = total + dk_got[by - 1].astype(f32)
        dk_v[...] = total.astype(bf)

    outs = [
        pltpu.make_async_copy(src, dst, out_l.at[i])
        for i, (src, dst) in enumerate(
            ((out_v, out_ref), (dq_v, dq_ref), (dk_v, dk_ref), (up_v, up_ref))
        )
    ]

    send_spans(0, 0, HK)
    for e in (4, 5, 2, 3, 6, 7, 1, 0):
        for j in range(2):
            x_share(e, j).start()
    loads[0].wait()
    build_bias(me, N_CTX, seg_ref, bias_ref)
    for load in loads[1:]:
        load.wait()

    probs(0, 4)
    sum_values(0)
    gather_values(0)
    sum_values(1)
    gather_values(1)
    send_spans(1, 0, 4)
    turn_inputs()
    pass_values(0)
    partials(0)
    pass_values(1)
    partials(1)
    grads(0, 2)
    sum_x(0)
    sum_x(1)
    grads(2, 3)
    adam(0)
    adam(1)
    grads(3, 4)
    outs[0].start()
    outs[1].start()
    pass_updates(0)
    pass_updates(1)
    sum_keys()
    outs[2].start()
    for h in range(2):
        for dx in range(1, N_X):
            for dh in range(N_ZH):
                along_x(h, dx, dh).wait_recv()
    outs[3].start()

    @pl.loop(0, HK)
    def _(g):
        for by in range(1, NB):
            halo(0, g, by).wait_send()
            halo(1, g, by).wait_send()
            dv_back(g, by).wait_send()
            dk_back(g, by).wait_send()

    for e in range(1, 8):
        for j in range(2):
            x_share(e, j).wait_send()
    for h in range(2):
        for dy in range(1, N_Y):
            vg_send(h, dy).wait_send()
        for dy in range(N_Y):
            vg_pass(h, dy).wait_send()
        for d in range(1, N_X):
            x_piece(h, d).wait_send()
        for e in range(1, 8):
            z_piece(h, e).wait_send()
        for dh in range(1, N_ZH):
            along_z(h, dh).wait_send()
        for dx in range(1, N_X):
            for dh in range(N_ZH):
                along_x(h, dx, dh).wait_send()
    for out in outs:
        out.wait()


PIECES = [(i, first, 32) for i in range(2) for first in range(0, BLK, 32)]
PIECES += [(2, 0, BLK)] + [(3, first, 128) for first in range(0, 512, 128)]


def hand_over_kernel(*refs):
    ins, outs, helds = refs[0:4], refs[4:8], refs[8:12]
    in_sems, out_sems = refs[12], refs[13]
    fetches, stores = [], []
    for n, (i, first, rows) in enumerate(PIECES):
        cut = pl.ds(first, rows)
        held = helds[i].at[cut, :]
        fetches.append(pltpu.make_async_copy(ins[i].at[cut, :], held, in_sems.at[n]))
        stores.append(pltpu.make_async_copy(held, outs[i].at[cut, :], out_sems.at[n]))
    for fetch in fetches:
        fetch.start()
    for fetch, store in zip(fetches, stores):
        fetch.wait()
        store.start()
    for store in stores:
        store.wait()


def body(
    layer_input, queries, layer_keys, layer_values, output_grad, segment_ids, first_moment, second_moment
):
    bf = jnp.bfloat16
    f32 = jnp.float32
    far = pl.BlockSpec(memory_space=pl.ANY)
    vmem = pltpu.VMEM
    dma = pltpu.SemaphoreType.DMA
    results = pl.pallas_call(
        step_kernel,
        out_shape=(
            jax.ShapeDtypeStruct(queries.shape, bf),
            jax.ShapeDtypeStruct(queries.shape, bf),
            jax.ShapeDtypeStruct(layer_keys.shape, bf),
            jax.ShapeDtypeStruct((N_CTX * ROWS, WIDTH), bf),
        ),
        in_specs=[far] * 8,
        out_specs=(far,) * 4,
        scratch_shapes=[
            vmem((BLK, HQ * HD), bf),
            vmem((BLK, HQ * HD), bf),
            vmem(segment_ids.shape, jnp.int32),
            vmem((ROWS, WIDTH), f32),
            vmem((ROWS, WIDTH), f32),
            vmem((SPAN, WIDE), f32),
            vmem((HK, SPAN, GROUP * HD), bf),
            vmem((SPAN, GROUP * HD), bf),
            vmem((BLK, HQ * HD), bf),
            vmem((BLK, HQ * HD), bf),
            vmem((SPAN, WIDTH), bf),
            vmem((SPAN, WIDTH), bf),
            vmem((SPAN, WIDTH), bf),
            vmem((SPAN, WIDTH), bf),
            vmem((NB - 1, BLK, WIDTH), bf),
            vmem((NB - 1, BLK, WIDTH), bf),
            vmem((8, BLK, 1024), bf),
            vmem((1024, 8 * BLK), bf),
            vmem((2, 8, BLK, HALF), bf),
            vmem((2, N_X, 256, HALF), bf),
            vmem((2, N_X, 256, HALF), bf),
            vmem((2, 256, HALF), f32),
            vmem((2, 256, HALF), bf),
            vmem((2, 8, ROWS, HALF), bf),
            vmem((N_CTX * ROWS, WIDTH), bf),
            vmem((BLK, WIDTH), bf),
            dma((7,)),
            dma((2, HK, NB - 1)),
            dma((2, HK, NB - 1)),
            dma((8, 2)),
            dma((8, 2)),
            dma((2,)),
            dma((HK, NB - 1)),
            dma((HK, NB - 1)),
            dma((HK, NB - 1)),
            dma((HK, NB - 1)),
            dma((2, 8)),
            dma((2, 8)),
            dma((2, N_X)),
            dma((2, N_X)),
            dma((2, 8)),
            dma((2, 8)),
            dma((2, N_X, N_ZH)),
            dma((2, N_X, N_ZH)),
            dma((4,)),
        ],
        compiler_params=pltpu.CompilerParams(
            collective_id=0, has_side_effects=True, vmem_limit_bytes=60 * 1024 * 1024
        ),
        cost_estimate=pl.CostEstimate(
            flops=2 * 6 * HQ * BLK * SPAN * HD,
            bytes_accessed=8 << 20,
            transcendentals=HQ * BLK * SPAN,
        ),
    )(
        layer_input, queries, layer_keys, layer_values, output_grad, segment_ids, first_moment,
        second_moment,
    )
    return pl.pallas_call(
        hand_over_kernel,
        out_shape=tuple(jax.ShapeDtypeStruct(part.shape, part.dtype) for part in results),
        in_specs=[far] * 4,
        out_specs=(far,) * 4,
        scratch_shapes=[vmem(part.shape, part.dtype) for part in results]
        + [dma((len(PIECES),)), dma((len(PIECES),))],
        compiler_params=pltpu.CompilerParams(vmem_limit_bytes=60 * 1024 * 1024),
        cost_estimate=pl.CostEstimate(flops=0, bytes_accessed=6 << 20, transcendentals=0),
    )(*results)


def solution(mesh):
    rows = P(("dp", "ctx"), None)
    in_specs = (rows, rows, rows, rows, rows, P("dp", None), rows, rows)
    out_specs = (rows, rows, rows, P("dp", None))
    return jax.shard_map(body, mesh=mesh, in_specs=in_specs, out_specs=out_specs, check_vma=False)
```

```python
import jax
import jax.numpy as jnp
from jax import lax
from jax.experimental import pallas as pl
from jax.experimental.pallas import tpu as pltpu
from jax.sharding import PartitionSpec as P

HQ = 32
HK = 4
HD = 128
GROUP = HQ // HK
BLK = 128
NB = 5
SPAN = NB * BLK
WIDE = 2 * HD
SCALE = HD**-0.5
LOG2E = 1.4426950408889634

first_fix = 1.0 - 0.9**8
second_fix = 1.0 - 0.999**8

NT = (((1,), (1,)), ((), ()))


def build_bias(me, n_ctx, seg_ref, bias_ref):
    rows = lax.broadcasted_iota(jnp.int32, (BLK, BLK), 0)
    cols = lax.broadcasted_iota(jnp.int32, (BLK, BLK), 1)
    own = seg_ref[0:1, pl.ds(pl.multiple_of(me * BLK, BLK), BLK)]
    for slot in range(NB):
        back = NB - 1 - slot
        block = lax.rem(me - back + n_ctx, n_ctx)
        theirs = seg_ref[0:1, pl.ds(pl.multiple_of(block * BLK, BLK), BLK)]
        column = jnp.sum(
            jnp.where(rows == cols, jnp.broadcast_to(theirs, (BLK, BLK)), 0).astype(jnp.float32),
            axis=1,
            keepdims=True,
        )
        allowed = column == own.astype(jnp.float32)
        if back == 0:
            allowed = allowed & (rows <= cols)
        else:
            allowed = allowed & (jnp.full((BLK, BLK), me, jnp.int32) >= back)
        bias = jnp.where(allowed, 0.0, -1e30)
        bias_ref[slot * BLK : (slot + 1) * BLK, 0:HD] = bias
        bias_ref[slot * BLK : (slot + 1) * BLK, HD:WIDE] = bias


def lanes(index):
    return pl.ds(pl.multiple_of(index * HD, HD), HD)


def pair_rows(ref, head):
    return jnp.concatenate([ref[:, lanes(head)], ref[:, lanes(head + 1)]], axis=0)


def group_rows(ref, g):
    return jnp.concatenate([ref[:, lanes(g * GROUP + i)] for i in range(GROUP)], axis=0)


def probs_of_group(g, q_ref, k_ref, bias_ref, prob_ref):
    k_head = k_ref[:, lanes(g)]
    for pair in range(GROUP // 2):
        head = g * GROUP + 2 * pair
        raw = lax.dot_general(
            k_head, pair_rows(q_ref, head), NT, preferred_element_type=jnp.float32
        )
        masked = raw + bias_ref[...]
        top = jnp.max(masked, axis=0, keepdims=True)
        grown = jnp.exp2((masked - top) * (SCALE * LOG2E))
        total = jnp.sum(grown, axis=0, keepdims=True)
        probs = grown * (1.0 / total)
        prob_ref[g, :, pair * WIDE : (pair + 1) * WIDE] = probs.astype(jnp.bfloat16)


def value_part(g, prob_ref, go_ref):
    return jnp.dot(prob_ref[g], group_rows(go_ref, g), preferred_element_type=jnp.float32)


def grads_of_group(g, q_ref, k_ref, v_ref, go_ref, prob_ref, ds_ref, out_ref, dq_ref):
    k_head = k_ref[:, lanes(g)]
    v_head = v_ref[:, lanes(g)]
    k_turned = k_head.T
    v_turned = v_head.T
    for pair in range(GROUP // 2):
        head = g * GROUP + 2 * pair
        cut = slice(pair * WIDE, (pair + 1) * WIDE)
        low = prob_ref[g, :, cut]
        dprobs = lax.dot_general(
            v_head, pair_rows(go_ref, head), NT, preferred_element_type=jnp.float32
        )
        probs = low.astype(jnp.float32)
        delta = jnp.sum(probs * dprobs, axis=0, keepdims=True)
        ds = (probs * (dprobs - delta)).astype(jnp.bfloat16)
        ds_ref[:, cut] = ds
        out_t = jnp.dot(v_turned, low, preferred_element_type=jnp.float32)
        dq_t = jnp.dot(k_turned, ds, preferred_element_type=jnp.float32) * SCALE
        for i in range(2):
            part = slice(i * HD, (i + 1) * HD)
            out_ref[:, lanes(head + i)] = out_t[:, part].T.astype(jnp.bfloat16)
            dq_ref[:, lanes(head + i)] = dq_t[:, part].T.astype(jnp.bfloat16)
    return (
        jnp.dot(ds_ref[...], group_rows(q_ref, g), preferred_element_type=jnp.float32) * SCALE
    )


MESH = pl.DeviceIdType.MESH
N_CTX = 16
N_X = 4
N_ZH = 4
N_Y = 4
ROWS = 32
WIDTH = HK * HD
HALF = WIDTH // 2


def remote(src, dst, send_sem, recv_sem, dp, ctx):
    return pltpu.make_async_remote_copy(
        src_ref=src,
        dst_ref=dst,
        send_sem=send_sem,
        recv_sem=recv_sem,
        device_id=(dp, ctx),
        device_id_type=MESH,
    )


def step_kernel(
    x_ref, q_hbm, k_hbm, v_hbm, go_hbm, seg_hbm, m_hbm, s_hbm,
    out_v, dq_v, dk_v, up_v,
    q_ref, go_ref, seg_ref, m_ref, s_ref,
    bias_ref, prob_ref, ds_ref, k_span, v_span, dv_part, dk_part, dv_got, dk_got,
    xs_ref, xt_ref, vg_ref, sx_ref, rx_ref, acc_ref, sz_ref, rz_ref,
    load_l, halo_s, halo_r, x_s, x_r, x_l, dv_s, dv_r, dk_s, dk_r, vg_s, vg_r,
    rx_s, rx_r, rz_s, rz_r, ag_s, ag_r,
):
    bf = jnp.bfloat16
    f32 = jnp.float32
    dp = lax.axis_index("dp")
    me = lax.axis_index("ctx")
    y, zl, core = dp // 4, (dp // 2) % 2, dp % 2
    x, zh = me // N_ZH, me % N_ZH
    own_rows = pl.ds((NB - 1) * BLK, BLK)

    loads = [
        pltpu.make_async_copy(src, dst, load_l.at[i])
        for i, (src, dst) in enumerate(
            (
                (seg_hbm, seg_ref),
                (k_hbm, k_span.at[own_rows, :]),
                (q_hbm, q_ref),
                (go_hbm, go_ref),
                (v_hbm, v_span.at[own_rows, :]),
                (m_hbm, m_ref),
                (s_hbm, s_ref),
            )
        )
    ]
    for load in loads:
        load.start()

    def ctx_at(by):
        return (me + by + N_CTX) % N_CTX

    def share_at(dy, dc):
        return ((y + dy) % N_Y) * 4 + zl * 2 + (core + dc) % 2

    def x_at(dx):
        return ((x + dx) % N_X) * N_ZH + zh

    def z_at(dh):
        return x * N_ZH + (zh + dh + N_ZH) % N_ZH

    def zl_at(dl):
        return y * 4 + ((zl + dl) % 2) * 2 + core

    partners = [(dp, ctx_at(by)) for by in (1, 2, 3, 4, -1, -2, -3, -4, 8)]
    partners += [(share_at(e // 2, e % 2), me) for e in range(1, 8)]
    partners += [(zl_at(1), z_at(dh)) for dh in range(N_ZH)]
    barrier = pltpu.get_barrier_semaphore()
    for partner in partners:
        pl.semaphore_signal(barrier, inc=1, device_id=partner, device_id_type=MESH)
    pl.semaphore_wait(barrier, len(partners))

    def halo(which, g, by):
        src, span = ((k_hbm, k_span), (v_hbm, v_span))[which]
        slot = NB - 1 - by
        return remote(
            src.at[:, lanes(g)],
            span.at[pl.ds(slot * BLK, BLK), lanes(g)],
            halo_s.at[which, g, by - 1],
            halo_r.at[which, g, by - 1],
            dp,
            ctx_at(by),
        )

    def x_share(e, j):
        dy, dc = e // 2, e % 2
        first = (((y + dy) % N_Y) * 4 + j * 2 + (core + dc) % 2) * 512
        src = x_ref.at[:, pl.ds(pl.multiple_of(first, 512), 512)]
        dst = xs_ref.at[e, :, pl.ds(j * 512, 512)]
        if e == 0:
            return pltpu.make_async_copy(src, dst, x_l.at[j])
        return remote(src, dst, x_s.at[e, j], x_r.at[e, j], share_at(dy, dc), me)

    def back(part, got, send, recv, g, by):
        slot = NB - 1 - by
        return remote(
            part.at[pl.ds(slot * BLK, BLK), lanes(g)],
            got.at[by - 1, :, lanes(g)],
            send.at[g, by - 1],
            recv.at[g, by - 1],
            dp,
            ctx_at(-by),
        )

    def dv_back(g, by):
        return back(dv_part, dv_got, dv_s, dv_r, g, by)

    def dk_back(g, by):
        return back(dk_part, dk_got, dk_s, dk_r, g, by)

    def send_spans(which, first, last):
        @pl.loop(first, last)
        def _(g):
            for by in range(1, NB):
                halo(which, g, by).start()

    def probs(first, last):
        @pl.loop(first, last)
        def _(g):
            for by in range(1, NB):
                halo(0, g, by).wait_recv()
            probs_of_group(g, q_ref, k_span, bias_ref, prob_ref)
            dv_part[:, lanes(g)] = value_part(g, prob_ref, go_ref).astype(bf)
            for by in range(1, NB):
                dv_back(g, by).start()

    def send_keys(first, last):
        @pl.loop(first, last)
        def _(g):
            for by in range(1, NB):
                dk_back(g, by).start()

    def grads(first, last, send=True):
        @pl.loop(first, last)
        def _(g):
            for by in range(1, NB):
                halo(1, g, by).wait_recv()
            dk = grads_of_group(
                g, q_ref, k_span, v_span, go_ref, prob_ref, ds_ref, out_v, dq_v
            )
            dk_part[:, lanes(g)] = dk.astype(bf)
            if send:
                for by in range(1, NB):
                    dk_back(g, by).start()

    def columns(h):
        return pl.ds(h * HALF, HALF)

    def sum_values(h):
        for g in (2 * h, 2 * h + 1):
            for by in range(1, NB):
                dv_back(g, by).wait_recv()
        total = dv_part[own_rows, columns(h)].astype(f32)
        for by in range(1, NB):
            total = total + dv_got[by - 1, :, columns(h)].astype(f32)
        vg_ref[h, 0] = total.astype(bf)

    def vg_send(h, dy):
        e = 2 * dy
        return remote(
            vg_ref.at[h, 0], vg_ref.at[h, e], vg_s.at[h, e], vg_r.at[h, e], share_at(dy, 0), me
        )

    def vg_pass(h, dy):
        e = 2 * dy
        return remote(
            vg_ref.at[h, e],
            vg_ref.at[h, e + 1],
            vg_s.at[h, e + 1],
            vg_r.at[h, e + 1],
            share_at(0, 1),
            me,
        )

    def gather_values(h):
        for dy in (2, 1, 3):
            vg_send(h, dy).start()
        vg_pass(h, 0).start()

    def pass_values(h):
        for dy in (1, 3, 2):
            vg_send(h, dy).wait_recv()
            vg_pass(h, dy).start()

    def turn_inputs():
        for e in range(8):
            for j in range(2):
                if e == 0:
                    x_share(e, j).wait()
                else:
                    x_share(e, j).wait_recv()

        @pl.loop(0, 8)
        def _(e):
            xt_ref[:, lanes(e)] = xs_ref[e].T

    def x_piece(h, d):
        return remote(
            sx_ref.at[h, d], rx_ref.at[h, d], rx_s.at[h, d], rx_r.at[h, d], dp, x_at(d)
        )

    def partial_for(h, d):
        first = ((x + d) % N_X) * 128
        left = jnp.concatenate(
            [xt_ref[pl.ds(pl.multiple_of(j * 512 + first, 128), 128), :] for j in range(2)], axis=0
        )
        return jnp.dot(left, vg_ref[h].reshape(8 * BLK, HALF), preferred_element_type=f32)

    def partials(h):
        for dy in range(N_Y):
            vg_pass(h, dy).wait_recv()
        for d in (2, 1, 3):
            sx_ref[h, d] = partial_for(h, d).astype(bf)
            x_piece(h, d).start()
        acc_ref[h] = partial_for(h, 0)

    def z_rows(dl, dh):
        first = ((zl + dl) % 2) * 128 + ((zh + dh) % N_ZH) * ROWS
        return pl.ds(pl.multiple_of(first, ROWS), ROWS)

    def z_piece(h, e):
        dl, dh = e % 2, e // 2
        return remote(
            sz_ref.at[h, z_rows(dl, dh), :],
            rz_ref.at[h, e],
            rz_s.at[h, e],
            rz_r.at[h, e],
            zl_at(dl),
            z_at(dh),
        )

    def sum_x(h):
        for d in (1, 3, 2):
            x_piece(h, d).wait_recv()
        total = acc_ref[h]
        for d in range(1, N_X):
            total = total + rx_ref[h, d].astype(f32)
        acc_ref[h] = total
        sz_ref[h] = total.astype(bf)
        for e in (4, 5, 3, 2, 6, 7, 1):
            z_piece(h, e).start()

    def up_rows(h, dh):
        return up_v.at[pl.ds(pl.multiple_of(z_at(dh) * ROWS, ROWS), ROWS), columns(h)]

    def along_z(h, dh):
        return remote(
            up_rows(h, 0), up_rows(h, 0), ag_s.at[h, 0, dh], ag_r.at[h, 0, dh], dp, z_at(dh)
        )

    def along_x(h, dx, dh):
        return remote(
            up_rows(h, -dh), up_rows(h, -dh), ag_s.at[h, dx, dh], ag_r.at[h, dx, dh], dp, x_at(dx)
        )

    def adam(h):
        for e in range(1, 8):
            z_piece(h, e).wait_recv()
        gradient = acc_ref[h, z_rows(0, 0), :]
        for e in range(1, 8):
            gradient = gradient + rz_ref[h, e].astype(f32)
        new_first = 0.9 * m_ref[:, columns(h)] + 0.1 * gradient
        new_second = 0.999 * s_ref[:, columns(h)] + 0.001 * gradient * gradient
        update = new_first / first_fix / (jnp.sqrt(new_second / second_fix) + 1e-08)
        up_v[pl.ds(pl.multiple_of(me * ROWS, ROWS), ROWS), columns(h)] = update.astype(bf)
        for dh in (2, 1, 3):
            along_z(h, dh).start()
        for dx in (2, 1, 3):
            along_x(h, dx, 0).start()

    def pass_updates(h):
        for dh in (1, 3, 2):
            along_z(h, dh).wait_recv()
            for dx in (2, 1, 3):
                along_x(h, dx, dh).start()

    def sum_keys():
        @pl.loop(0, HK)
        def _(g):
            for by in range(1, NB):
                dk_back(g, by).wait_recv()

        total = dk_part[own_rows, :].astype(f32)
        for by in range(1, NB):
            total = total + dk_got[by - 1].astype(f32)
        dk_v[...] = total.astype(bf)

    send_spans(0, 0, HK)
    for e in (4, 5, 2, 3, 6, 7, 1, 0):
        for j in range(2):
            x_share(e, j).start()
    loads[0].wait()
    build_bias(me, N_CTX, seg_ref, bias_ref)
    for load in loads[1:]:
        load.wait()

    probs(0, 4)
    sum_values(0)
    gather_values(0)
    sum_values(1)
    gather_values(1)
    send_spans(1, 0, 4)
    turn_inputs()
    pass_values(0)
    partials(0)
    pass_values(1)
    partials(1)
    grads(0, 3)
    sum_x(0)
    sum_x(1)
    grads(3, 4, False)
    adam(0)
    adam(1)
    send_keys(3, 4)
    pass_updates(0)
    pass_updates(1)
    sum_keys()
    for h in range(2):
        for dx in range(1, N_X):
            for dh in range(N_ZH):
                along_x(h, dx, dh).wait_recv()

    @pl.loop(0, HK)
    def _(g):
        for by in range(1, NB):
            halo(0, g, by).wait_send()
            halo(1, g, by).wait_send()
            dv_back(g, by).wait_send()
            dk_back(g, by).wait_send()

    for e in range(1, 8):
        for j in range(2):
            x_share(e, j).wait_send()
    for h in range(2):
        for dy in range(1, N_Y):
            vg_send(h, dy).wait_send()
        for dy in range(N_Y):
            vg_pass(h, dy).wait_send()
        for d in range(1, N_X):
            x_piece(h, d).wait_send()
        for e in range(1, 8):
            z_piece(h, e).wait_send()
        for dh in range(1, N_ZH):
            along_z(h, dh).wait_send()
        for dx in range(1, N_X):
            for dh in range(N_ZH):
                along_x(h, dx, dh).wait_send()


PIECES = [(i, first, 32) for i in range(2) for first in range(0, BLK, 32)]
PIECES += [(2, 0, BLK)] + [(3, first, 128) for first in range(0, 512, 128)]


def hand_over_kernel(*refs):
    copies = [
        pltpu.make_async_copy(
            refs[i].at[pl.ds(first, rows), :], refs[4 + i].at[pl.ds(first, rows), :], refs[8].at[n]
        )
        for n, (i, first, rows) in enumerate(PIECES)
    ]
    for copy in copies:
        copy.start()
    for copy in copies:
        copy.wait()


def body(
    layer_input, queries, layer_keys, layer_values, output_grad, segment_ids, first_moment, second_moment
):
    bf = jnp.bfloat16
    f32 = jnp.float32
    far = pl.BlockSpec(memory_space=pl.ANY)
    near = pl.BlockSpec(memory_space=pltpu.VMEM)
    hbm = pl.BlockSpec(memory_space=pltpu.HBM)
    vmem = pltpu.VMEM
    dma = pltpu.SemaphoreType.DMA
    results = pl.pallas_call(
        step_kernel,
        out_shape=(
            vmem(queries.shape, bf),
            vmem(queries.shape, bf),
            vmem(layer_keys.shape, bf),
            vmem((N_CTX * ROWS, WIDTH), bf),
        ),
        in_specs=[hbm] * 8,
        out_specs=(near,) * 4,
        scratch_shapes=[
            vmem((BLK, HQ * HD), bf),
            vmem((BLK, HQ * HD), bf),
            vmem(segment_ids.shape, jnp.int32),
            vmem((ROWS, WIDTH), f32),
            vmem((ROWS, WIDTH), f32),
            vmem((SPAN, WIDE), f32),
            vmem((HK, SPAN, GROUP * HD), bf),
            vmem((SPAN, GROUP * HD), bf),
            vmem((SPAN, WIDTH), bf),
            vmem((SPAN, WIDTH), bf),
            vmem((SPAN, WIDTH), bf),
            vmem((SPAN, WIDTH), bf),
            vmem((NB - 1, BLK, WIDTH), bf),
            vmem((NB - 1, BLK, WIDTH), bf),
            vmem((8, BLK, 1024), bf),
            vmem((1024, 8 * BLK), bf),
            vmem((2, 8, BLK, HALF), bf),
            vmem((2, N_X, 256, HALF), bf),
            vmem((2, N_X, 256, HALF), bf),
            vmem((2, 256, HALF), f32),
            vmem((2, 256, HALF), bf),
            vmem((2, 8, ROWS, HALF), bf),
            dma((7,)),
            dma((2, HK, NB - 1)),
            dma((2, HK, NB - 1)),
            dma((8, 2)),
            dma((8, 2)),
            dma((2,)),
            dma((HK, NB - 1)),
            dma((HK, NB - 1)),
            dma((HK, NB - 1)),
            dma((HK, NB - 1)),
            dma((2, 8)),
            dma((2, 8)),
            dma((2, N_X)),
            dma((2, N_X)),
            dma((2, 8)),
            dma((2, 8)),
            dma((2, N_X, N_ZH)),
            dma((2, N_X, N_ZH)),
        ],
        compiler_params=pltpu.CompilerParams(
            collective_id=0, has_side_effects=True, vmem_limit_bytes=56 * 1024 * 1024
        ),
        cost_estimate=pl.CostEstimate(
            flops=2 * 6 * HQ * BLK * SPAN * HD,
            bytes_accessed=8 << 20,
            transcendentals=HQ * BLK * SPAN,
        ),
    )(
        layer_input, queries, layer_keys, layer_values, output_grad, segment_ids, first_moment,
        second_moment,
    )
    return pl.pallas_call(
        hand_over_kernel,
        out_shape=tuple(jax.ShapeDtypeStruct(part.shape, part.dtype) for part in results),
        in_specs=[near] * 4,
        out_specs=(far,) * 4,
        scratch_shapes=[dma((len(PIECES),))],
        compiler_params=pltpu.CompilerParams(vmem_limit_bytes=60 * 1024 * 1024),
        cost_estimate=pl.CostEstimate(flops=0, bytes_accessed=6 << 20, transcendentals=0),
    )(*[pltpu.with_memory_space_constraint(part, pltpu.VMEM) for part in results])


def solution(mesh):
    rows = P(("dp", "ctx"), None)
    in_specs = (rows, rows, rows, rows, rows, P("dp", None), rows, rows)
    out_specs = (rows, rows, rows, P("dp", None))
    return jax.shard_map(body, mesh=mesh, in_specs=in_specs, out_specs=out_specs, check_vma=False)
```

```python
import jax
import jax.numpy as jnp
from jax import lax
from jax.experimental import pallas as pl
from jax.experimental.pallas import tpu as pltpu
from jax.sharding import PartitionSpec as P

HQ = 32
HK = 4
HD = 128
GROUP = HQ // HK
BLK = 128
NB = 5
SPAN = NB * BLK
WIDE = 2 * HD
SCALE = HD**-0.5
LOG2E = 1.4426950408889634

first_fix = 1.0 - 0.9**8
second_fix = 1.0 - 0.999**8

NT = (((1,), (1,)), ((), ()))


def build_bias(me, n_ctx, seg_ref, bias_ref):
    rows = lax.broadcasted_iota(jnp.int32, (BLK, BLK), 0)
    cols = lax.broadcasted_iota(jnp.int32, (BLK, BLK), 1)
    own = seg_ref[0:1, pl.ds(pl.multiple_of(me * BLK, BLK), BLK)]
    for slot in range(NB):
        back = NB - 1 - slot
        block = lax.rem(me - back + n_ctx, n_ctx)
        theirs = seg_ref[0:1, pl.ds(pl.multiple_of(block * BLK, BLK), BLK)]
        column = jnp.sum(
            jnp.where(rows == cols, jnp.broadcast_to(theirs, (BLK, BLK)), 0).astype(jnp.float32),
            axis=1,
            keepdims=True,
        )
        allowed = column == own.astype(jnp.float32)
        if back == 0:
            allowed = allowed & (rows <= cols)
        else:
            allowed = allowed & (jnp.full((BLK, BLK), me, jnp.int32) >= back)
        bias = jnp.where(allowed, 0.0, -1e30)
        bias_ref[slot * BLK : (slot + 1) * BLK, 0:HD] = bias
        bias_ref[slot * BLK : (slot + 1) * BLK, HD:WIDE] = bias


def lanes(index):
    return pl.ds(pl.multiple_of(index * HD, HD), HD)


def pair_rows(ref, head):
    return jnp.concatenate([ref[:, lanes(head)], ref[:, lanes(head + 1)]], axis=0)


def group_rows(ref, g):
    return jnp.concatenate([ref[:, lanes(g * GROUP + i)] for i in range(GROUP)], axis=0)


def probs_of_group(g, q_ref, k_ref, bias_ref, prob_ref):
    k_head = k_ref[:, lanes(g)]
    for pair in range(GROUP // 2):
        head = g * GROUP + 2 * pair
        raw = lax.dot_general(
            k_head, pair_rows(q_ref, head), NT, preferred_element_type=jnp.float32
        )
        masked = raw + bias_ref[...]
        top = jnp.max(masked, axis=0, keepdims=True)
        grown = jnp.exp2((masked - top) * (SCALE * LOG2E))
        total = jnp.sum(grown, axis=0, keepdims=True)
        probs = grown * (1.0 / total)
        prob_ref[g, :, pair * WIDE : (pair + 1) * WIDE] = probs.astype(jnp.bfloat16)


def value_part(g, prob_ref, go_ref):
    return jnp.dot(prob_ref[g], group_rows(go_ref, g), preferred_element_type=jnp.float32)


def grads_of_group(g, q_ref, k_ref, v_ref, go_ref, prob_ref, ds_ref, out_ref, dq_ref):
    k_head = k_ref[:, lanes(g)]
    v_head = v_ref[:, lanes(g)]
    k_turned = k_head.T
    v_turned = v_head.T
    for pair in range(GROUP // 2):
        head = g * GROUP + 2 * pair
        cut = slice(pair * WIDE, (pair + 1) * WIDE)
        low = prob_ref[g, :, cut]
        dprobs = lax.dot_general(
            v_head, pair_rows(go_ref, head), NT, preferred_element_type=jnp.float32
        )
        probs = low.astype(jnp.float32)
        delta = jnp.sum(probs * dprobs, axis=0, keepdims=True)
        ds = (probs * (dprobs - delta)).astype(jnp.bfloat16)
        ds_ref[:, cut] = ds
        out_t = jnp.dot(v_turned, low, preferred_element_type=jnp.float32)
        dq_t = jnp.dot(k_turned, ds, preferred_element_type=jnp.float32) * SCALE
        for i in range(2):
            part = slice(i * HD, (i + 1) * HD)
            out_ref[:, lanes(head + i)] = out_t[:, part].T.astype(jnp.bfloat16)
            dq_ref[:, lanes(head + i)] = dq_t[:, part].T.astype(jnp.bfloat16)
    return (
        jnp.dot(ds_ref[...], group_rows(q_ref, g), preferred_element_type=jnp.float32) * SCALE
    )


MESH = pl.DeviceIdType.MESH
N_CTX = 16
N_X = 4
N_ZH = 4
N_Y = 4
ROWS = 32
WIDTH = HK * HD
HALF = WIDTH // 2


def remote(src, dst, send_sem, recv_sem, dp, ctx):
    return pltpu.make_async_remote_copy(
        src_ref=src,
        dst_ref=dst,
        send_sem=send_sem,
        recv_sem=recv_sem,
        device_id=(dp, ctx),
        device_id_type=MESH,
    )


def step_kernel(
    x_ref, q_hbm, k_hbm, v_hbm, go_hbm, seg_hbm, m_hbm, s_hbm,
    out_v, dq_v, dk_v, up_v,
    q_ref, go_ref, seg_ref, m_ref, s_ref,
    bias_ref, prob_ref, ds_ref, k_span, v_span, dv_part, dk_part, dv_got, dk_got,
    xs_ref, xt_ref, vg_ref, sx_ref, rx_ref, acc_ref, sz_ref, rz_ref,
    load_l, halo_s, halo_r, x_s, x_r, x_l, dv_s, dv_r, dk_s, dk_r, vg_s, vg_r,
    rx_s, rx_r, rz_s, rz_r, ag_s, ag_r,
):
    bf = jnp.bfloat16
    f32 = jnp.float32
    dp = lax.axis_index("dp")
    me = lax.axis_index("ctx")
    y, zl, core = dp // 4, (dp // 2) % 2, dp % 2
    x, zh = me // N_ZH, me % N_ZH
    own_rows = pl.ds((NB - 1) * BLK, BLK)

    loads = [
        pltpu.make_async_copy(src, dst, load_l.at[i])
        for i, (src, dst) in enumerate(
            (
                (seg_hbm, seg_ref),
                (k_hbm, k_span.at[own_rows, :]),
                (q_hbm, q_ref),
                (go_hbm, go_ref),
                (v_hbm, v_span.at[own_rows, :]),
                (m_hbm, m_ref),
                (s_hbm, s_ref),
            )
        )
    ]
    for load in loads:
        load.start()

    def ctx_at(by):
        return (me + by + N_CTX) % N_CTX

    def share_at(dy, dc):
        return ((y + dy) % N_Y) * 4 + zl * 2 + (core + dc) % 2

    def x_at(dx):
        return ((x + dx) % N_X) * N_ZH + zh

    def z_at(dh):
        return x * N_ZH + (zh + dh + N_ZH) % N_ZH

    def zl_at(dl):
        return y * 4 + ((zl + dl) % 2) * 2 + core

    partners = [(dp, ctx_at(by)) for by in (1, 2, 3, 4, -1, -2, -3, -4, 8)]
    partners += [(share_at(e // 2, e % 2), me) for e in range(1, 8)]
    partners += [(zl_at(1), z_at(dh)) for dh in range(N_ZH)]
    barrier = pltpu.get_barrier_semaphore()
    for partner in partners:
        pl.semaphore_signal(barrier, inc=1, device_id=partner, device_id_type=MESH)
    pl.semaphore_wait(barrier, len(partners))

    def halo(which, g, by):
        src, span = ((k_hbm, k_span), (v_hbm, v_span))[which]
        slot = NB - 1 - by
        if which == 1 and by < N_ZH:
            first = (1 - (zh + by) // N_ZH) * ((NB - 1) * BLK)
            return remote(
                v_span.at[pl.ds(pl.multiple_of(first, BLK), BLK), lanes(g)],
                v_span.at[pl.ds(slot * BLK, BLK), lanes(g)],
                halo_s.at[which, g, by - 1],
                halo_r.at[which, g, by - 1],
                dp,
                z_at(by),
            )
        return remote(
            src.at[:, lanes(g)],
            span.at[pl.ds(slot * BLK, BLK), lanes(g)],
            halo_s.at[which, g, by - 1],
            halo_r.at[which, g, by - 1],
            dp,
            ctx_at(by),
        )

    def x_share(e, j):
        dy, dc = e // 2, e % 2
        first = (((y + dy) % N_Y) * 4 + j * 2 + (core + dc) % 2) * 512
        src = x_ref.at[:, pl.ds(pl.multiple_of(first, 512), 512)]
        dst = xs_ref.at[e, :, pl.ds(j * 512, 512)]
        if e == 0:
            return pltpu.make_async_copy(src, dst, x_l.at[j])
        return remote(src, dst, x_s.at[e, j], x_r.at[e, j], share_at(dy, dc), me)

    def back(part, got, send, recv, g, by):
        slot = NB - 1 - by
        return remote(
            part.at[pl.ds(slot * BLK, BLK), lanes(g)],
            got.at[by - 1, :, lanes(g)],
            send.at[g, by - 1],
            recv.at[g, by - 1],
            dp,
            ctx_at(-by),
        )

    def dv_back(g, by):
        return back(dv_part, dv_got, dv_s, dv_r, g, by)

    def dk_back(g, by):
        return back(dk_part, dk_got, dk_s, dk_r, g, by)

    def send_keys_on():
        @pl.loop(0, HK)
        def _(g):
            for by in range(1, NB):
                halo(0, g, by).start()

    def send_values_on():
        @pl.loop(0, HK)
        def _(g):
            halo(1, g, NB - 1).start()

    def spread_values(first, last):
        @pl.loop(first, last)
        def _(g):
            halo(1, g, NB - 1).wait_recv()
            for by in range(1, N_ZH):
                halo(1, g, by).start()

    def probs(first, last):
        @pl.loop(first, last)
        def _(g):
            for by in range(1, NB):
                halo(0, g, by).wait_recv()
            probs_of_group(g, q_ref, k_span, bias_ref, prob_ref)
            dv_part[:, lanes(g)] = value_part(g, prob_ref, go_ref).astype(bf)
            for by in range(1, NB):
                dv_back(g, by).start()

    def send_keys(first, last):
        @pl.loop(first, last)
        def _(g):
            for by in range(1, NB):
                dk_back(g, by).start()

    def grads(first, last, send=True):
        @pl.loop(first, last)
        def _(g):
            for by in range(1, N_ZH):
                halo(1, g, by).wait_recv()
            dk = grads_of_group(
                g, q_ref, k_span, v_span, go_ref, prob_ref, ds_ref, out_v, dq_v
            )
            dk_part[:, lanes(g)] = dk.astype(bf)
            if send:
                for by in range(1, NB):
                    dk_back(g, by).start()

    def columns(h):
        return pl.ds(h * HALF, HALF)

    def sum_values(h):
        for g in (2 * h, 2 * h + 1):
            for by in range(1, NB):
                dv_back(g, by).wait_recv()
        total = dv_part[own_rows, columns(h)].astype(f32)
        for by in range(1, NB):
            total = total + dv_got[by - 1, :, columns(h)].astype(f32)
        vg_ref[h, 0] = total.astype(bf)

    def vg_send(h, dy):
        e = 2 * dy
        return remote(
            vg_ref.at[h, 0], vg_ref.at[h, e], vg_s.at[h, e], vg_r.at[h, e], share_at(dy, 0), me
        )

    def vg_pass(h, dy):
        e = 2 * dy
        return remote(
            vg_ref.at[h, e],
            vg_ref.at[h, e + 1],
            vg_s.at[h, e + 1],
            vg_r.at[h, e + 1],
            share_at(0, 1),
            me,
        )

    def gather_values(h):
        for dy in (2, 1, 3):
            vg_send(h, dy).start()
        vg_pass(h, 0).start()

    def pass_values(h):
        for dy in (1, 3, 2):
            vg_send(h, dy).wait_recv()
            vg_pass(h, dy).start()

    def turn_inputs():
        for e in range(8):
            for j in range(2):
                if e == 0:
                    x_share(e, j).wait()
                else:
                    x_share(e, j).wait_recv()

        @pl.loop(0, 8)
        def _(e):
            xt_ref[:, lanes(e)] = xs_ref[e].T

    def x_piece(h, d):
        return remote(
            sx_ref.at[h, d], rx_ref.at[h, d], rx_s.at[h, d], rx_r.at[h, d], dp, x_at(d)
        )

    def partial_for(h, d):
        first = ((x + d) % N_X) * 128
        left = jnp.concatenate(
            [xt_ref[pl.ds(pl.multiple_of(j * 512 + first, 128), 128), :] for j in range(2)], axis=0
        )
        return jnp.dot(left, vg_ref[h].reshape(8 * BLK, HALF), preferred_element_type=f32)

    def partials(h):
        for dy in range(N_Y):
            vg_pass(h, dy).wait_recv()
        for d in (2, 1, 3):
            sx_ref[h, d] = partial_for(h, d).astype(bf)
            x_piece(h, d).start()
        acc_ref[h] = partial_for(h, 0)

    def z_rows(dl, dh):
        first = ((zl + dl) % 2) * 128 + ((zh + dh) % N_ZH) * ROWS
        return pl.ds(pl.multiple_of(first, ROWS), ROWS)

    def z_piece(h, e):
        dl, dh = e % 2, e // 2
        return remote(
            sz_ref.at[h, z_rows(dl, dh), :],
            rz_ref.at[h, e],
            rz_s.at[h, e],
            rz_r.at[h, e],
            zl_at(dl),
            z_at(dh),
        )

    def sum_x(h):
        for d in (1, 3, 2):
            x_piece(h, d).wait_recv()
        total = acc_ref[h]
        for d in range(1, N_X):
            total = total + rx_ref[h, d].astype(f32)
        acc_ref[h] = total
        sz_ref[h] = total.astype(bf)
        for e in (4, 5, 3, 2, 6, 7, 1):
            z_piece(h, e).start()

    def up_rows(h, dh):
        return up_v.at[pl.ds(pl.multiple_of(z_at(dh) * ROWS, ROWS), ROWS), columns(h)]

    def along_z(h, dh):
        return remote(
            up_rows(h, 0), up_rows(h, 0), ag_s.at[h, 0, dh], ag_r.at[h, 0, dh], dp, z_at(dh)
        )

    def along_x(h, dx, dh):
        return remote(
            up_rows(h, -dh), up_rows(h, -dh), ag_s.at[h, dx, dh], ag_r.at[h, dx, dh], dp, x_at(dx)
        )

    def adam(h):
        for e in range(1, 8):
            z_piece(h, e).wait_recv()
        gradient = acc_ref[h, z_rows(0, 0), :]
        for e in range(1, 8):
            gradient = gradient + rz_ref[h, e].astype(f32)
        new_first = 0.9 * m_ref[:, columns(h)] + 0.1 * gradient
        new_second = 0.999 * s_ref[:, columns(h)] + 0.001 * gradient * gradient
        update = new_first / first_fix / (jnp.sqrt(new_second / second_fix) + 1e-08)
        up_v[pl.ds(pl.multiple_of(me * ROWS, ROWS), ROWS), columns(h)] = update.astype(bf)
        for dh in (2, 1, 3):
            along_z(h, dh).start()
        for dx in (2, 1, 3):
            along_x(h, dx, 0).start()

    def pass_updates(h):
        for dh in (1, 3, 2):
            along_z(h, dh).wait_recv()
            for dx in (2, 1, 3):
                along_x(h, dx, dh).start()

    def sum_keys():
        @pl.loop(0, HK)
        def _(g):
            for by in range(1, NB):
                dk_back(g, by).wait_recv()

        total = dk_part[own_rows, :].astype(f32)
        for by in range(1, NB):
            total = total + dk_got[by - 1].astype(f32)
        dk_v[...] = total.astype(bf)

    send_keys_on()
    send_values_on()
    for e in (4, 5, 2, 3, 6, 7, 1, 0):
        for j in range(2):
            x_share(e, j).start()
    loads[0].wait()
    build_bias(me, N_CTX, seg_ref, bias_ref)
    for load in loads[1:]:
        load.wait()

    probs(0, 4)
    sum_values(0)
    gather_values(0)
    sum_values(1)
    gather_values(1)
    spread_values(0, 4)
    turn_inputs()
    pass_values(0)
    partials(0)
    pass_values(1)
    partials(1)
    grads(0, 2)
    sum_x(0)
    grads(2, 3)
    sum_x(1)
    grads(3, 4, False)
    adam(0)
    adam(1)
    send_keys(3, 4)
    pass_updates(0)
    pass_updates(1)
    sum_keys()
    for h in range(2):
        for dx in range(1, N_X):
            for dh in range(N_ZH):
                along_x(h, dx, dh).wait_recv()

    @pl.loop(0, HK)
    def _(g):
        for by in range(1, NB):
            halo(0, g, by).wait_send()
            halo(1, g, by).wait_send()
            dv_back(g, by).wait_send()
            dk_back(g, by).wait_send()

    for e in range(1, 8):
        for j in range(2):
            x_share(e, j).wait_send()
    for h in range(2):
        for dy in range(1, N_Y):
            vg_send(h, dy).wait_send()
        for dy in range(N_Y):
            vg_pass(h, dy).wait_send()
        for d in range(1, N_X):
            x_piece(h, d).wait_send()
        for e in range(1, 8):
            z_piece(h, e).wait_send()
        for dh in range(1, N_ZH):
            along_z(h, dh).wait_send()
        for dx in range(1, N_X):
            for dh in range(N_ZH):
                along_x(h, dx, dh).wait_send()


PIECES = [(i, first, 32) for i in range(2) for first in range(0, BLK, 32)]
PIECES += [(2, 0, BLK)] + [(3, first, 128) for first in range(0, 512, 128)]


def hand_over_kernel(*refs):
    copies = [
        pltpu.make_async_copy(
            refs[i].at[pl.ds(first, rows), :], refs[4 + i].at[pl.ds(first, rows), :], refs[8].at[n]
        )
        for n, (i, first, rows) in enumerate(PIECES)
    ]
    for copy in copies:
        copy.start()
    for copy in copies:
        copy.wait()


def body(
    layer_input, queries, layer_keys, layer_values, output_grad, segment_ids, first_moment, second_moment
):
    bf = jnp.bfloat16
    f32 = jnp.float32
    far = pl.BlockSpec(memory_space=pl.ANY)
    near = pl.BlockSpec(memory_space=pltpu.VMEM)
    hbm = pl.BlockSpec(memory_space=pltpu.HBM)
    vmem = pltpu.VMEM
    dma = pltpu.SemaphoreType.DMA
    results = pl.pallas_call(
        step_kernel,
        out_shape=(
            vmem(queries.shape, bf),
            vmem(queries.shape, bf),
            vmem(layer_keys.shape, bf),
            vmem((N_CTX * ROWS, WIDTH), bf),
        ),
        in_specs=[hbm] * 8,
        out_specs=(near,) * 4,
        scratch_shapes=[
            vmem((BLK, HQ * HD), bf),
            vmem((BLK, HQ * HD), bf),
            vmem(segment_ids.shape, jnp.int32),
            vmem((ROWS, WIDTH), f32),
            vmem((ROWS, WIDTH), f32),
            vmem((SPAN, WIDE), f32),
            vmem((HK, SPAN, GROUP * HD), bf),
            vmem((SPAN, GROUP * HD), bf),
            vmem((SPAN, WIDTH), bf),
            vmem((SPAN, WIDTH), bf),
            vmem((SPAN, WIDTH), bf),
            vmem((SPAN, WIDTH), bf),
            vmem((NB - 1, BLK, WIDTH), bf),
            vmem((NB - 1, BLK, WIDTH), bf),
            vmem((8, BLK, 1024), bf),
            vmem((1024, 8 * BLK), bf),
            vmem((2, 8, BLK, HALF), bf),
            vmem((2, N_X, 256, HALF), bf),
            vmem((2, N_X, 256, HALF), bf),
            vmem((2, 256, HALF), f32),
            vmem((2, 256, HALF), bf),
            vmem((2, 8, ROWS, HALF), bf),
            dma((7,)),
            dma((2, HK, NB - 1)),
            dma((2, HK, NB - 1)),
            dma((8, 2)),
            dma((8, 2)),
            dma((2,)),
            dma((HK, NB - 1)),
            dma((HK, NB - 1)),
            dma((HK, NB - 1)),
            dma((HK, NB - 1)),
            dma((2, 8)),
            dma((2, 8)),
            dma((2, N_X)),
            dma((2, N_X)),
            dma((2, 8)),
            dma((2, 8)),
            dma((2, N_X, N_ZH)),
            dma((2, N_X, N_ZH)),
        ],
        compiler_params=pltpu.CompilerParams(
            collective_id=0, has_side_effects=True, vmem_limit_bytes=56 * 1024 * 1024
        ),
        cost_estimate=pl.CostEstimate(
            flops=2 * 6 * HQ * BLK * SPAN * HD,
            bytes_accessed=8 << 20,
            transcendentals=HQ * BLK * SPAN,
        ),
    )(
        layer_input, queries, layer_keys, layer_values, output_grad, segment_ids, first_moment,
        second_moment,
    )
    return pl.pallas_call(
        hand_over_kernel,
        out_shape=tuple(jax.ShapeDtypeStruct(part.shape, part.dtype) for part in results),
        in_specs=[near] * 4,
        out_specs=(far,) * 4,
        scratch_shapes=[dma((len(PIECES),))],
        compiler_params=pltpu.CompilerParams(vmem_limit_bytes=60 * 1024 * 1024),
        cost_estimate=pl.CostEstimate(flops=0, bytes_accessed=6 << 20, transcendentals=0),
    )(*[pltpu.with_memory_space_constraint(part, pltpu.VMEM) for part in results])


def solution(mesh):
    rows = P(("dp", "ctx"), None)
    in_specs = (rows, rows, rows, rows, rows, P("dp", None), rows, rows)
    out_specs = (rows, rows, rows, P("dp", None))
    return jax.shard_map(body, mesh=mesh, in_specs=in_specs, out_specs=out_specs, check_vma=False)
```

```python
import jax
import jax.numpy as jnp
from jax import lax
from jax.experimental import pallas as pl
from jax.experimental.pallas import tpu as pltpu
from jax.sharding import PartitionSpec as P

HQ = 32
HK = 4
HD = 128
GROUP = HQ // HK
BLK = 128
NB = 5
SPAN = NB * BLK
WIDE = 2 * HD
SCALE = HD**-0.5
LOG2E = 1.4426950408889634

first_fix = 1.0 - 0.9**8
second_fix = 1.0 - 0.999**8

NT = (((1,), (1,)), ((), ()))


def build_bias(me, n_ctx, seg_ref, bias_ref):
    rows = lax.broadcasted_iota(jnp.int32, (BLK, BLK), 0)
    cols = lax.broadcasted_iota(jnp.int32, (BLK, BLK), 1)
    own = seg_ref[0:1, pl.ds(pl.multiple_of(me * BLK, BLK), BLK)]
    for slot in range(NB):
        back = NB - 1 - slot
        block = lax.rem(me - back + n_ctx, n_ctx)
        theirs = seg_ref[0:1, pl.ds(pl.multiple_of(block * BLK, BLK), BLK)]
        column = jnp.sum(
            jnp.where(rows == cols, jnp.broadcast_to(theirs, (BLK, BLK)), 0).astype(jnp.float32),
            axis=1,
            keepdims=True,
        )
        allowed = column == own.astype(jnp.float32)
        if back == 0:
            allowed = allowed & (rows <= cols)
        else:
            allowed = allowed & (jnp.full((BLK, BLK), me, jnp.int32) >= back)
        bias = jnp.where(allowed, 0.0, -1e30)
        bias_ref[slot * BLK : (slot + 1) * BLK, 0:HD] = bias
        bias_ref[slot * BLK : (slot + 1) * BLK, HD:WIDE] = bias


def lanes(index):
    return pl.ds(pl.multiple_of(index * HD, HD), HD)


def pair_rows(ref, head):
    return jnp.concatenate([ref[:, lanes(head)], ref[:, lanes(head + 1)]], axis=0)


def group_rows(ref, g):
    return jnp.concatenate([ref[:, lanes(g * GROUP + i)] for i in range(GROUP)], axis=0)


def probs_of_group(g, q_ref, k_ref, bias_ref, prob_ref):
    k_head = k_ref[:, lanes(g)]
    for pair in range(GROUP // 2):
        head = g * GROUP + 2 * pair
        raw = lax.dot_general(
            k_head, pair_rows(q_ref, head), NT, preferred_element_type=jnp.float32
        )
        masked = raw + bias_ref[...]
        top = jnp.max(masked, axis=0, keepdims=True)
        grown = jnp.exp2((masked - top) * (SCALE * LOG2E))
        total = jnp.sum(grown, axis=0, keepdims=True)
        probs = grown * (1.0 / total)
        prob_ref[g, :, pair * WIDE : (pair + 1) * WIDE] = probs.astype(jnp.bfloat16)


def value_part(g, prob_ref, go_ref):
    return jnp.dot(prob_ref[g], group_rows(go_ref, g), preferred_element_type=jnp.float32)


def grads_of_group(g, q_ref, k_ref, v_ref, go_ref, prob_ref, ds_ref, out_ref, dq_ref):
    k_head = k_ref[:, lanes(g)]
    v_head = v_ref[:, lanes(g)]
    k_turned = k_head.T
    v_turned = v_head.T
    for pair in range(GROUP // 2):
        head = g * GROUP + 2 * pair
        cut = slice(pair * WIDE, (pair + 1) * WIDE)
        low = prob_ref[g, :, cut]
        dprobs = lax.dot_general(
            v_head, pair_rows(go_ref, head), NT, preferred_element_type=jnp.float32
        )
        probs = low.astype(jnp.float32)
        delta = jnp.sum(probs * dprobs, axis=0, keepdims=True)
        ds = (probs * (dprobs - delta)).astype(jnp.bfloat16)
        ds_ref[:, cut] = ds
        out_t = jnp.dot(v_turned, low, preferred_element_type=jnp.float32)
        dq_t = jnp.dot(k_turned, ds, preferred_element_type=jnp.float32) * SCALE
        for i in range(2):
            part = slice(i * HD, (i + 1) * HD)
            out_ref[:, lanes(head + i)] = out_t[:, part].T.astype(jnp.bfloat16)
            dq_ref[:, lanes(head + i)] = dq_t[:, part].T.astype(jnp.bfloat16)
    return (
        jnp.dot(ds_ref[...], group_rows(q_ref, g), preferred_element_type=jnp.float32) * SCALE
    )


MESH = pl.DeviceIdType.MESH
N_CTX = 16
N_X = 4
N_ZH = 4
N_Y = 4
ROWS = 32
WIDTH = HK * HD
HALF = WIDTH // 2


def remote(src, dst, send_sem, recv_sem, dp, ctx):
    return pltpu.make_async_remote_copy(
        src_ref=src,
        dst_ref=dst,
        send_sem=send_sem,
        recv_sem=recv_sem,
        device_id=(dp, ctx),
        device_id_type=MESH,
    )


def step_kernel(
    x_ref, q_hbm, k_hbm, v_hbm, go_hbm, seg_hbm, m_hbm, s_hbm,
    out_v, dq_v, dk_v, up_v,
    q_ref, go_ref, seg_ref, m_ref, s_ref,
    bias_ref, prob_ref, ds_ref, k_span, v_span, dv_part, dk_part, dv_got, dk_got,
    xs_ref, xt_ref, vg_ref, part_ref, sx_ref, rx_ref, acc_ref, sz_ref, rz_ref,
    load_l, halo_s, halo_r, x_s, x_r, x_l, dv_s, dv_r, dk_s, dk_r, vg_s, vg_r,
    rx_s, rx_r, rz_s, rz_r, ag_s, ag_r,
):
    bf = jnp.bfloat16
    f32 = jnp.float32
    dp = lax.axis_index("dp")
    me = lax.axis_index("ctx")
    y, zl, core = dp // 4, (dp // 2) % 2, dp % 2
    x, zh = me // N_ZH, me % N_ZH
    own_rows = pl.ds((NB - 1) * BLK, BLK)

    loads = [
        pltpu.make_async_copy(src, dst, load_l.at[i])
        for i, (src, dst) in enumerate(
            (
                (seg_hbm, seg_ref),
                (k_hbm, k_span.at[own_rows, :]),
                (q_hbm, q_ref),
                (go_hbm, go_ref),
                (v_hbm, v_span.at[own_rows, :]),
                (m_hbm, m_ref),
                (s_hbm, s_ref),
            )
        )
    ]
    for load in loads:
        load.start()

    def ctx_at(by):
        return (me + by + N_CTX) % N_CTX

    def share_at(dy, dc):
        return ((y + dy) % N_Y) * 4 + zl * 2 + (core + dc) % 2

    def x_at(dx):
        return ((x + dx) % N_X) * N_ZH + zh

    def z_at(dh):
        return x * N_ZH + (zh + dh + N_ZH) % N_ZH

    def zl_at(dl):
        return y * 4 + ((zl + dl) % 2) * 2 + core

    partners = [(dp, ctx_at(by)) for by in (1, 2, 3, 4, -1, -2, -3, -4, 8)]
    partners += [(share_at(e // 2, e % 2), me) for e in range(1, 8)]
    partners += [(zl_at(1), z_at(dh)) for dh in range(N_ZH)]
    partners += [(share_at(0, 1), x_at(dx)) for dx in range(1, N_X)]
    barrier = pltpu.get_barrier_semaphore()
    for partner in partners:
        pl.semaphore_signal(barrier, inc=1, device_id=partner, device_id_type=MESH)
    pl.semaphore_wait(barrier, len(partners))

    def halo(which, g, by):
        src, span = ((k_hbm, k_span), (v_hbm, v_span))[which]
        slot = NB - 1 - by
        if which == 1 and by < N_ZH:
            first = (1 - (zh + by) // N_ZH) * ((NB - 1) * BLK)
            return remote(
                v_span.at[pl.ds(pl.multiple_of(first, BLK), BLK), lanes(g)],
                v_span.at[pl.ds(slot * BLK, BLK), lanes(g)],
                halo_s.at[which, g, by - 1],
                halo_r.at[which, g, by - 1],
                dp,
                z_at(by),
            )
        return remote(
            src.at[:, lanes(g)],
            span.at[pl.ds(slot * BLK, BLK), lanes(g)],
            halo_s.at[which, g, by - 1],
            halo_r.at[which, g, by - 1],
            dp,
            ctx_at(by),
        )

    def peer_at(p, by, dc):
        if p == 0:
            return share_at(by, dc), me
        return share_at(0, dc), x_at(by)

    def x_share(p, e, n):
        by, dc = e // 2, e % 2
        other = (core + dc) % 2
        if p == 0:
            first, size = ((y + by) % N_Y * 4 + other) * 512, 512
        else:
            first, size = (n * 4 + 2 + other) * 512 + (x + by) % N_X * 128, 128
        src = x_ref.at[:, pl.ds(pl.multiple_of(first, size), size)]
        dst = xs_ref.at[p, e, :, pl.ds(n * size, size)]
        if e == 0:
            return pltpu.make_async_copy(src, dst, x_l.at[p, n])
        return remote(src, dst, x_s.at[p, e, n], x_r.at[p, e, n], *peer_at(p, by, dc))

    SHARES = [(0, e, 0) for e in (4, 5, 2, 3, 6, 7, 1, 0)]
    SHARES += [(1, e, n) for e in (4, 5, 2, 3, 6, 7, 1, 0) for n in range(N_Y)]

    def back(part, got, send, recv, g, by):
        slot = NB - 1 - by
        return remote(
            part.at[pl.ds(slot * BLK, BLK), lanes(g)],
            got.at[by - 1, :, lanes(g)],
            send.at[g, by - 1],
            recv.at[g, by - 1],
            dp,
            ctx_at(-by),
        )

    def dv_back(g, by):
        return back(dv_part, dv_got, dv_s, dv_r, g, by)

    def dk_back(g, by):
        return back(dk_part, dk_got, dk_s, dk_r, g, by)

    def send_keys_on():
        @pl.loop(0, HK)
        def _(g):
            for by in range(1, NB):
                halo(0, g, by).start()

    def send_values_on():
        @pl.loop(0, HK)
        def _(g):
            halo(1, g, NB - 1).start()

    def spread_values(first, last):
        @pl.loop(first, last)
        def _(g):
            halo(1, g, NB - 1).wait_recv()
            for by in range(1, N_ZH):
                halo(1, g, by).start()

    def probs(first, last):
        @pl.loop(first, last)
        def _(g):
            for by in range(1, NB):
                halo(0, g, by).wait_recv()
            probs_of_group(g, q_ref, k_span, bias_ref, prob_ref)
            dv_part[:, lanes(g)] = value_part(g, prob_ref, go_ref).astype(bf)
            for by in range(1, NB):
                dv_back(g, by).start()

    def send_keys(first, last):
        @pl.loop(first, last)
        def _(g):
            for by in range(1, NB):
                dk_back(g, by).start()

    def grads(first, last, send=True):
        @pl.loop(first, last)
        def _(g):
            for by in range(1, N_ZH):
                halo(1, g, by).wait_recv()
            dk = grads_of_group(
                g, q_ref, k_span, v_span, go_ref, prob_ref, ds_ref, out_v, dq_v
            )
            dk_part[:, lanes(g)] = dk.astype(bf)
            if send:
                for by in range(1, NB):
                    dk_back(g, by).start()

    def columns(h):
        return pl.ds(h * HALF, HALF)

    def sum_values(h):
        for g in (2 * h, 2 * h + 1):
            for by in range(1, NB):
                dv_back(g, by).wait_recv()
        total = dv_part[own_rows, columns(h)].astype(f32)
        for by in range(1, NB):
            total = total + dv_got[by - 1, :, columns(h)].astype(f32)
        vg_ref[0, h, 0] = total.astype(bf)
        vg_ref[1, h, 0] = total.astype(bf)

    def vg_send(p, h, by):
        e = 2 * by
        return remote(
            vg_ref.at[p, h, 0],
            vg_ref.at[p, h, e],
            vg_s.at[p, h, e],
            vg_r.at[p, h, e],
            *peer_at(p, by, 0),
        )

    def vg_pass(p, h, by):
        e = 2 * by
        return remote(
            vg_ref.at[p, h, e],
            vg_ref.at[p, h, e + 1],
            vg_s.at[p, h, e + 1],
            vg_r.at[p, h, e + 1],
            *peer_at(p, 0, 1),
        )

    def gather_values(h):
        for by in (2, 1, 3):
            for p in range(2):
                vg_send(p, h, by).start()
        for p in range(2):
            vg_pass(p, h, 0).start()

    def pass_values(h):
        for by in (1, 3, 2):
            for p in range(2):
                vg_send(p, h, by).wait_recv()
                vg_pass(p, h, by).start()

    def send_inputs(which):
        for share in SHARES:
            if share[0] == which:
                x_share(*share).start()

    def turn_inputs(which):
        for p, e, n in SHARES:
            if p != which:
                continue
            if e == 0:
                x_share(p, e, n).wait()
            else:
                x_share(p, e, n).wait_recv()

        @pl.loop(0, 8)
        def _(e):
            xt_ref[which, :, lanes(e)] = xs_ref[which, e].T

    def piece_rows(p, d):
        place = (x + d) % N_X if p == 0 else (y + d) % N_Y
        return pl.ds(pl.multiple_of(place * 128, 128), 128)

    def x_piece(p, h, d):
        return remote(
            sx_ref.at[p, h, piece_rows(p, d), :],
            rx_ref.at[p, h, d],
            rx_s.at[p, h, d],
            rx_r.at[p, h, d],
            *((dp, x_at(d)) if p == 0 else (share_at(d, 0), me)),
        )

    def partials(h):
        for p in range(2):
            for by in range(N_Y):
                vg_pass(p, h, by).wait_recv()
            partial = jnp.dot(
                xt_ref[p], vg_ref[p, h].reshape(8 * BLK, HALF), preferred_element_type=f32
            )
            part_ref[p, h] = partial
            sx_ref[p, h] = partial.astype(bf)
            for d in (2, 1, 3):
                x_piece(p, h, d).start()

    def z_rows(dl, dh):
        first = ((zl + dl) % 2) * 128 + ((zh + dh) % N_ZH) * ROWS
        return pl.ds(pl.multiple_of(first, ROWS), ROWS)

    def z_piece(h, e):
        dl, dh = e % 2, e // 2
        return remote(
            sz_ref.at[h, z_rows(dl, dh), :],
            rz_ref.at[h, e],
            rz_s.at[h, e],
            rz_r.at[h, e],
            zl_at(dl),
            z_at(dh),
        )

    def sum_x(h):
        for p in range(2):
            for d in (1, 3, 2):
                x_piece(p, h, d).wait_recv()
            total = part_ref[p, h, piece_rows(p, 0), :]
            for d in range(1, N_X):
                total = total + rx_ref[p, h, d].astype(f32)
            acc_ref[h, p * 128 : (p + 1) * 128, :] = total
            sz_ref[h, p * 128 : (p + 1) * 128, :] = total.astype(bf)
        for e in (4, 5, 3, 2, 6, 7, 1):
            z_piece(h, e).start()

    def up_rows(h, dh):
        return up_v.at[pl.ds(pl.multiple_of(z_at(dh) * ROWS, ROWS), ROWS), columns(h)]

    def along_z(h, dh):
        return remote(
            up_rows(h, 0), up_rows(h, 0), ag_s.at[h, 0, dh], ag_r.at[h, 0, dh], dp, z_at(dh)
        )

    def along_x(h, dx, dh):
        return remote(
            up_rows(h, -dh), up_rows(h, -dh), ag_s.at[h, dx, dh], ag_r.at[h, dx, dh], dp, x_at(dx)
        )

    def adam(h):
        for e in range(1, 8):
            z_piece(h, e).wait_recv()
        gradient = acc_ref[h, z_rows(0, 0), :]
        for e in range(1, 8):
            gradient = gradient + rz_ref[h, e].astype(f32)
        new_first = 0.9 * m_ref[:, columns(h)] + 0.1 * gradient
        new_second = 0.999 * s_ref[:, columns(h)] + 0.001 * gradient * gradient
        update = new_first / first_fix / (jnp.sqrt(new_second / second_fix) + 1e-08)
        up_v[pl.ds(pl.multiple_of(me * ROWS, ROWS), ROWS), columns(h)] = update.astype(bf)
        for dh in (2, 1, 3):
            along_z(h, dh).start()
        for dx in (2, 1, 3):
            along_x(h, dx, 0).start()

    def pass_updates(h):
        for dh in (1, 3, 2):
            along_z(h, dh).wait_recv()
            for dx in (2, 1, 3):
                along_x(h, dx, dh).start()

    def sum_keys():
        @pl.loop(0, HK)
        def _(g):
            for by in range(1, NB):
                dk_back(g, by).wait_recv()

        total = dk_part[own_rows, :].astype(f32)
        for by in range(1, NB):
            total = total + dk_got[by - 1].astype(f32)
        dk_v[...] = total.astype(bf)

    send_keys_on()
    send_values_on()
    loads[0].wait()
    build_bias(me, N_CTX, seg_ref, bias_ref)
    for load in loads[1:]:
        load.wait()

    send_inputs(0)
    send_inputs(1)
    probs(0, 4)
    sum_values(0)
    gather_values(0)
    sum_values(1)
    gather_values(1)
    spread_values(0, 4)
    turn_inputs(0)
    turn_inputs(1)
    pass_values(0)
    partials(0)
    pass_values(1)
    partials(1)
    grads(0, 2)
    sum_x(0)
    grads(2, 3)
    sum_x(1)
    grads(3, 4, False)
    adam(0)
    adam(1)
    send_keys(3, 4)
    pass_updates(0)
    pass_updates(1)
    sum_keys()
    for h in range(2):
        for dx in range(1, N_X):
            for dh in range(N_ZH):
                along_x(h, dx, dh).wait_recv()

    @pl.loop(0, HK)
    def _(g):
        for by in range(1, NB):
            halo(0, g, by).wait_send()
            halo(1, g, by).wait_send()
            dv_back(g, by).wait_send()
            dk_back(g, by).wait_send()

    for p, e, n in SHARES:
        if e:
            x_share(p, e, n).wait_send()
    for h in range(2):
        for p in range(2):
            for by in range(1, N_Y):
                vg_send(p, h, by).wait_send()
            for by in range(N_Y):
                vg_pass(p, h, by).wait_send()
            for d in range(1, N_X):
                x_piece(p, h, d).wait_send()
        for e in range(1, 8):
            z_piece(h, e).wait_send()
        for dh in range(1, N_ZH):
            along_z(h, dh).wait_send()
        for dx in range(1, N_X):
            for dh in range(N_ZH):
                along_x(h, dx, dh).wait_send()


PIECES = [(i, first, 32) for i in range(2) for first in range(0, BLK, 32)]
PIECES += [(2, 0, BLK)] + [(3, first, 128) for first in range(0, 512, 128)]


def hand_over_kernel(*refs):
    copies = [
        pltpu.make_async_copy(
            refs[i].at[pl.ds(first, rows), :], refs[4 + i].at[pl.ds(first, rows), :], refs[8].at[n]
        )
        for n, (i, first, rows) in enumerate(PIECES)
    ]
    for copy in copies:
        copy.start()
    for copy in copies:
        copy.wait()


def body(
    layer_input, queries, layer_keys, layer_values, output_grad, segment_ids, first_moment, second_moment
):
    bf = jnp.bfloat16
    f32 = jnp.float32
    far = pl.BlockSpec(memory_space=pl.ANY)
    near = pl.BlockSpec(memory_space=pltpu.VMEM)
    hbm = pl.BlockSpec(memory_space=pltpu.HBM)
    vmem = pltpu.VMEM
    dma = pltpu.SemaphoreType.DMA
    results = pl.pallas_call(
        step_kernel,
        out_shape=(
            vmem(queries.shape, bf),
            vmem(queries.shape, bf),
            vmem(layer_keys.shape, bf),
            vmem((N_CTX * ROWS, WIDTH), bf),
        ),
        in_specs=[hbm] * 8,
        out_specs=(near,) * 4,
        scratch_shapes=[
            vmem((BLK, HQ * HD), bf),
            vmem((BLK, HQ * HD), bf),
            vmem(segment_ids.shape, jnp.int32),
            vmem((ROWS, WIDTH), f32),
            vmem((ROWS, WIDTH), f32),
            vmem((SPAN, WIDE), f32),
            vmem((HK, SPAN, GROUP * HD), bf),
            vmem((SPAN, GROUP * HD), bf),
            vmem((SPAN, WIDTH), bf),
            vmem((SPAN, WIDTH), bf),
            vmem((SPAN, WIDTH), bf),
            vmem((SPAN, WIDTH), bf),
            vmem((NB - 1, BLK, WIDTH), bf),
            vmem((NB - 1, BLK, WIDTH), bf),
            vmem((2, 8, BLK, 512), bf),
            vmem((2, 512, 8 * BLK), bf),
            vmem((2, 2, 8, BLK, HALF), bf),
            vmem((2, 2, 512, HALF), f32),
            vmem((2, 2, 512, HALF), bf),
            vmem((2, 2, N_X, 128, HALF), bf),
            vmem((2, 256, HALF), f32),
            vmem((2, 256, HALF), bf),
            vmem((2, 8, ROWS, HALF), bf),
            dma((7,)),
            dma((2, HK, NB - 1)),
            dma((2, HK, NB - 1)),
            dma((2, 8, N_Y)),
            dma((2, 8, N_Y)),
            dma((2, N_Y)),
            dma((HK, NB - 1)),
            dma((HK, NB - 1)),
            dma((HK, NB - 1)),
            dma((HK, NB - 1)),
            dma((2, 2, 8)),
            dma((2, 2, 8)),
            dma((2, 2, N_X)),
            dma((2, 2, N_X)),
            dma((2, 8)),
            dma((2, 8)),
            dma((2, N_X, N_ZH)),
            dma((2, N_X, N_ZH)),
        ],
        compiler_params=pltpu.CompilerParams(
            collective_id=0, has_side_effects=True, vmem_limit_bytes=56 * 1024 * 1024
        ),
        cost_estimate=pl.CostEstimate(
            flops=2 * 6 * HQ * BLK * SPAN * HD,
            bytes_accessed=8 << 20,
            transcendentals=HQ * BLK * SPAN,
        ),
    )(
        layer_input, queries, layer_keys, layer_values, output_grad, segment_ids, first_moment,
        second_moment,
    )
    return pl.pallas_call(
        hand_over_kernel,
        out_shape=tuple(jax.ShapeDtypeStruct(part.shape, part.dtype) for part in results),
        in_specs=[near] * 4,
        out_specs=(far,) * 4,
        scratch_shapes=[dma((len(PIECES),))],
        compiler_params=pltpu.CompilerParams(vmem_limit_bytes=60 * 1024 * 1024),
        cost_estimate=pl.CostEstimate(flops=0, bytes_accessed=6 << 20, transcendentals=0),
    )(*[pltpu.with_memory_space_constraint(part, pltpu.VMEM) for part in results])


def solution(mesh):
    rows = P(("dp", "ctx"), None)
    in_specs = (rows, rows, rows, rows, rows, P("dp", None), rows, rows)
    out_specs = (rows, rows, rows, P("dp", None))
    return jax.shard_map(body, mesh=mesh, in_specs=in_specs, out_specs=out_specs, check_vma=False)
```
